256 devices in a mesh: rows: 128 (over z, x, y), pair: 2 (over core).
Axes of the slice: x: 4, y: 4, z: 8, core: 2. Of those that a mesh axis runs over, the one named last changes fastest.
Arguments:
- a_blocks: bfloat16 [6144, 27, 4096], P(('rows', 'pair')), may hold values from -0.15625 to 0.15625
- a_cols: int32 [6144, 27], P(('rows', 'pair')), may hold values from 0 to 6143, as said below
- slots: int32 [6144, 27], P(('rows', 'pair')), may hold values from 0 to 7
- prolong: bfloat16 [6144, 4096], P(('rows', 'pair')), may hold values from -1.5 to 1.5
- aggregate: int32 [6144], P(('rows', 'pair')), may hold values from 0 to 511, as said below
- owner: int32 [32768, 1], P('rows'), may hold values from 0 to 127; in each aligned block of 256 rows (0 to 255, 256 to 511, ...) at most 4 rows name the same one
Outputs:
- agglomerated: float32 [128, 128, 4, 512], P('rows')
The draws below stay inside these ranges and needn't reach their ends.
Inputs may be any that keep to these rules, and one draw needn't show every extreme that they name: a_cols[f, 0] = f, and a_cols[f, k] // 24 differs from f // 24 by at most one; the blocks of each existing neighbour (one at the first and last device) are named. aggregate[f] // 4 = f // 48; every coarse block is named. Among the 256 coarse rows of one chip, no owner is named by more than 4 rows, a bound that some block reaches.
All inputs are finite; a program needn't handle non-finite values.
Results may differ from the reference program's by a relative error of at most 0.0029.
Values may be sent and summed in bfloat16 or wider, within the bound.
A program may use at most 128 MiB of HBM per device.

```python
import math
import jax
import jax.numpy as jnp
import numpy as np
from jax import lax

BS = 64
KA = 27
KC = 8
FB_DEV = 24
CB_DEV = 4
NF = 6144
NC = 512
MOST = 4
N_ROWS = 128
N_PAIR = 2


def draw_a_cols(key, part):
    key = jax.random.fold_in(key, 11)
    fine_ids = jnp.arange(NF, dtype=jnp.int32)
    offsets = jax.random.randint(key, (NF, KA), -FB_DEV, 2 * FB_DEV, dtype=jnp.int32)
    columns = (fine_ids // FB_DEV * FB_DEV)[:, None] + offsets
    columns = jnp.clip(columns, 0, NF - 1)
    position = jnp.arange(KA, dtype=jnp.int32)[None, :]
    return jnp.where(position == 0, fine_ids[:, None], columns).astype(jnp.int32)


def draw_aggregate(key, part):
    key = jax.random.fold_in(key, 23)
    fine_ids = jnp.arange(NF, dtype=jnp.int32)
    chip_index = fine_ids // (2 * FB_DEV)
    local_ids = fine_ids % (2 * FB_DEV)
    picks = jax.random.randint(key, (NF,), 0, CB_DEV, dtype=jnp.int32)
    return (chip_index * CB_DEV + jnp.where(local_ids < CB_DEV, local_ids, picks)).astype(jnp.int32)


def with_ends(values, stream_key, least, largest):
    place = [jax.random.randint(jax.random.fold_in(stream_key, axis), (), 0, length) for axis, length in enumerate(values.shape)]
    main_axis = values.shape.index(max(values.shape))
    next_to = place[:main_axis] + [(place[main_axis] + 1) % values.shape[main_axis]] + place[main_axis + 1:]
    return values.at[tuple(place)].set(least).at[tuple(next_to)].set(largest)


def levels(own_key, dims, split, least, high):
    factor_of = 1.0
    for dim, parts in split:
        steps = jax.random.uniform(jax.random.fold_in(jax.random.fold_in(own_key, 6), dim), (parts,), jnp.float32, least / len(split), high / len(split))
        factor_of = factor_of * jnp.repeat(jnp.exp(steps), dims[dim] // parts).reshape((-1,) + (1,) * (len(dims) - 1 - dim))
    return factor_of


def routed_block(own_key, own, number, rows, amount, top, limit, skew):
    ranking = jax.random.permutation(own_key, amount)
    crowded, ordinary = shares(amount, rows * top, limit, skew, True), shares(amount, rows * top, limit, skew, False)
    places = jnp.arange(amount)

    def named(lengths, offset_by):
        used = int((lengths > 0).sum())
        fixed = max(1, used // 4)
        shifted = fixed + (places - fixed + offset_by * (used - fixed)) % max(1, amount - fixed)
        return jnp.zeros((amount,), jnp.int32).at[ranking[jnp.where(places < fixed, places, shifted)]].set(jnp.asarray(lengths, jnp.int32))

    lengths = jnp.where(number % 4 == 0, named(crowded, number // 4), named(ordinary, number - number // 4 - 1))
    mixed = jax.random.permutation(jax.random.fold_in(own, 3), amount)
    donor, sink = mixed[0:amount // 2 * 2:2], mixed[1:amount // 2 * 2:2]
    room = jnp.minimum(lengths[donor] - 1, limit - lengths[sink]) // 2
    room = jnp.where((donor == ranking[0]) | (sink == ranking[0]) | (lengths[sink] == 0), 0, jnp.maximum(room, 0))
    shifted = jax.random.randint(jax.random.fold_in(own, 4), (amount // 2,), 0, 1 << 20) % (room + 1)
    lengths = lengths.at[donor].add(-shifted).at[sink].add(shifted)
    members = jnp.searchsorted(jnp.cumsum(lengths), jnp.arange(rows * top), side="right").astype(jnp.int32)
    listing = members.reshape(top, rows).T
    listing = listing[jax.random.permutation(jax.random.fold_in(own, 1), rows)]
    offset_by = jax.random.randint(jax.random.fold_in(own, 2), (rows, 1), 0, top)
    return jnp.take_along_axis(listing, (jnp.arange(top)[None, :] + offset_by) % top, axis=1)


def shares(number_of, total, bound, slope, full):
    weights = [(1 << 20) // math.isqrt(standing ** slope) + 1 for standing in range(1, number_of + 1)]
    largest = bound if full else min(bound, max(-(-total // number_of), total * weights[0] // sum(weights)))
    least = 1 if total - largest >= number_of - 1 else 0
    given, spare = [largest] + [least] * (number_of - 1), total - largest - least * (number_of - 1)
    while spare > 0:
        movable = [i for i in range(1, number_of) if given[i] < largest] or [i for i in range(1, number_of) if given[i] < bound]
        mass, budget = sum([weights[i] for i in movable]), spare
        for i in movable:
            extra = min(bound - given[i], max(1, budget * weights[i] // mass), spare)
            given[i] = given[i] + extra
            spare = spare - extra
    return np.array(given)


def noise(own_key, shape, scale, limit, split=(), held_as=jnp.bfloat16):
    values = scale * jax.random.normal(own_key, shape, jnp.float32)
    if split:
        values = values * levels(own_key, shape, split, -0.22, 0.18)
    return jnp.clip(values, -limit, limit).astype(held_as)


def setup_inputs(seed: int = 0) -> dict:
    arg_keys = jax.random.split(jax.random.key(seed), 7)
    a_blocks = noise(arg_keys[0], (NF, KA, BS * BS), (BS * KA) ** -0.5, 0.15625, ((0, 256),))
    a_cols = draw_a_cols(jax.random.fold_in(arg_keys[6], 71), 0)
    slots = with_ends(jax.random.randint(arg_keys[2], (NF, KA), 0, KC), jax.random.fold_in(arg_keys[2], 1), 0, KC - 1).astype(jnp.int32)
    prolong = noise(arg_keys[3], (NF, BS * BS), 0.25, 1.5, ((0, 256),))
    aggregate = draw_aggregate(jax.random.fold_in(arg_keys[6], 71), 0)
    owner_keys = jax.random.split(jax.random.fold_in(arg_keys[5], 1), (NC * BS) // (CB_DEV * BS))
    owner_turns = jax.random.permutation(jax.random.fold_in(arg_keys[5], 3), (NC * BS) // (CB_DEV * BS))
    owner = jax.vmap(lambda own, number: routed_block(jax.random.fold_in(arg_keys[5], 2), own, number, CB_DEV * BS, N_ROWS, 1, MOST, 2))(owner_keys, owner_turns).reshape((NC * BS, 1))
    return dict(a_blocks=a_blocks, a_cols=a_cols, slots=slots, prolong=prolong, aggregate=aggregate, owner=owner)


def reference(a_blocks, a_cols, slots, prolong, aggregate, owner):
    device_count = N_ROWS * N_PAIR
    highest = lax.Precision.HIGHEST
    prolong_square = prolong.reshape(NF, BS, BS)

    def device_term(inputs):
        blocks_here, cols_here, slots_here, prolong_here, agg_here, device = inputs
        picked = prolong_square[cols_here]
        product = jnp.einsum("fkij,fkjl->fkil", blocks_here.astype(jnp.float32), picked.astype(jnp.float32), precision=highest)
        slot_onehot = (slots_here[..., None] == jnp.arange(KC, dtype=jnp.int32)).astype(jnp.float32)
        summed = jnp.einsum("fks,fkil->fsil", slot_onehot, product, precision=highest).astype(jnp.bfloat16)
        galerkin = jnp.einsum("fja,fsjb->fasb", prolong_here.astype(jnp.float32), summed.astype(jnp.float32), precision=highest)
        local_agg = agg_here - (device // N_PAIR) * CB_DEV
        member = (local_agg[:, None] == jnp.arange(CB_DEV, dtype=jnp.int32)).astype(jnp.float32)
        return jnp.einsum("fc,fasb->casb", member, galerkin, precision=highest)

    terms = lax.map(device_term, (
        a_blocks.reshape(device_count, FB_DEV, KA, BS, BS),
        a_cols.reshape(device_count, FB_DEV, KA),
        slots.reshape(device_count, FB_DEV, KA),
        prolong_square.reshape(device_count, FB_DEV, BS, BS),
        aggregate.reshape(device_count, FB_DEV),
        jnp.arange(device_count, dtype=jnp.int32)))
    coarse = terms.reshape(N_ROWS, N_PAIR, CB_DEV * BS, KC * BS).sum(axis=1)
    dest_ids = owner[:, 0].reshape(N_ROWS, CB_DEV * BS)
    target = (dest_ids[..., None] == jnp.arange(N_ROWS, dtype=jnp.int32)).astype(jnp.int32)
    earlier = jnp.cumsum(target, axis=1) - target
    rank_slot = jnp.sum(earlier * target, axis=2).astype(jnp.int32)
    source = jnp.broadcast_to(jnp.arange(N_ROWS, dtype=jnp.int32)[:, None], dest_ids.shape)
    result = jnp.zeros((N_ROWS, N_ROWS, MOST, KC * BS), jnp.float32)
    return result.at[dest_ids, source, rank_slot].set(coarse)
```

```python
import functools

import jax
import jax.numpy as jnp
from jax import lax
from jax.experimental import pallas as pl
from jax.experimental.pallas import tpu as pltpu
from jax.sharding import PartitionSpec as P

BS = 64
KA = 27
KC = 8
FB = 24
CB = 4
MOST = 4
ROWS = CB * BS
COLS = KC * BS
HALF = COLS // 2
KT = 7
CHUNKS = 4
DIMS = (8, 4, 4)
MESH = pl.DeviceIdType.MESH
BF16 = jnp.bfloat16
F32 = jnp.float32


def kernel(
    dims,
    a_hbm,
    cols_ref,
    slots_ref,
    prolong_hbm,
    agg_ref,
    owner_ref,
    out_ref,
    a_ref,
    praw,
    stage,
    nat,
    left,
    window,
    masks,
    qperm,
    turned,
    summed,
    onehot,
    part,
    theirs,
    outbox,
    a_sem,
    p_sem,
    near_send,
    near_recv,
    pair_send,
    pair_recv,
    out_send,
    one_send,
    out_recv,
    fwd_send,
    fwd_recv,
    y_sem,
    x_sem,
):
    nz, nx, ny = dims
    chips = nz * nx * ny
    half = chips // 2
    chip = lax.axis_index("rows")
    core = lax.axis_index("pair")
    other = 1 - core
    z, x, y = chip // (nx * ny), (chip // ny) % nx, chip % ny
    beyond = (chip + chips - 1 + 2 * core) % chips

    per = FB // CHUNKS
    fetches = [
        pltpu.make_async_copy(
            a_hbm.at[pl.ds(i * per, per)], a_ref.at[pl.ds(i * per, per)], a_sem.at[i]
        )
        for i in range(CHUNKS)
    ]
    own = pltpu.make_async_copy(prolong_hbm, praw.at[1], p_sem)
    own.start()
    for fetch in fetches:
        fetch.start()

    y_ring = [(z * nx + x) * ny + (y + i) % ny for i in range(1, ny)]
    x_ring = [(z * nx + (x + i) % nx) * ny + y for i in range(1, nx)]
    z_ring = [(((z + i) % nz) * nx + x) * ny + y for i in range(1, nz)]
    barrier = pltpu.get_barrier_semaphore()
    met = [(chip, other), (beyond, other)] + [(c, core) for c in y_ring + x_ring + z_ring]
    for device in met:
        pl.semaphore_signal(barrier, inc=1, device_id=device, device_id_type=MESH)
    own.wait()
    pl.semaphore_wait(barrier, len(met))

    to_partner = pltpu.make_async_remote_copy(
        src_ref=praw.at[1],
        dst_ref=praw.at[2 * core],
        send_sem=near_send.at[0],
        recv_sem=near_recv.at[0],
        device_id=(chip, other),
        device_id_type=MESH,
    )
    to_beyond = pltpu.make_async_remote_copy(
        src_ref=praw.at[1],
        dst_ref=praw.at[2 * other],
        send_sem=near_send.at[1],
        recv_sem=near_recv.at[1],
        device_id=(beyond, other),
        device_id_type=MESH,
    )
    to_beyond.start()
    to_partner.start()
    for c in y_ring:
        pl.semaphore_signal(y_sem, inc=1, device_id=(c, core), device_id_type=MESH)

    lane = lax.broadcasted_iota(jnp.int32, (32, 128), 1)
    low = lane < BS

    column_slot = lax.broadcasted_iota(jnp.int32, (16, COLS), 1) // BS
    for s in range(KC):
        masks[s] = jnp.where(column_slot == s, 1.0, 0.0).astype(BF16)

    owner_col = owner_ref[...]
    owners = jnp.broadcast_to(owner_col, (ROWS, 128))
    target = jnp.where(
        owners == lax.broadcasted_iota(jnp.int32, (ROWS, 128), 1), 1.0, 0.0
    )
    earlier = jnp.where(
        lax.broadcasted_iota(jnp.int32, (ROWS, ROWS), 0)
        > lax.broadcasted_iota(jnp.int32, (ROWS, ROWS), 1),
        1.0,
        0.0,
    ).astype(BF16)
    before = jnp.dot(earlier, target.astype(BF16), preferred_element_type=F32)
    rank = jnp.sum(before * target, axis=1, keepdims=True)
    key = jnp.broadcast_to(owner_col.astype(F32) * MOST + rank, (ROWS, 128))
    key_row = jnp.transpose(key)[0:1, :]
    side = (chip // half + core) % 2
    row_id = lax.broadcasted_iota(jnp.int32, (256, ROWS), 0)
    for i in range(half * 16 // 256 if half >= 16 else 1):
        n = min(256, half * 16)
        rid = row_id[:n] + i * 256
        code = (side * half + rid // 16) * MOST + rid % MOST
        onehot[pl.ds(i * 256, n), :] = jnp.where(code.astype(F32) == key_row, 1.0, 0.0).astype(BF16)

    def relay_a(f, carry):
        for t in range(32):
            stage[pl.ds(t * 32, KA), :] = a_ref[f, :, pl.ds(t * 128, 128)].astype(F32)
        for g in range(14):
            one = stage[pl.ds(2 * g, 32, stride=32), :]
            if 2 * g + 1 < KA:
                two = stage[pl.ds(2 * g + 1, 32, stride=32), :]
            else:
                two = jnp.zeros_like(one)
            top = jnp.where(low, one, pltpu.roll(two, BS, 1))
            bottom = jnp.where(low, pltpu.roll(one, BS, 1), two)
            left[f, pl.ds(0, 32), pl.ds(g * 128, 128)] = top.astype(BF16)
            left[f, pl.ds(32, 32), pl.ds(g * 128, 128)] = bottom.astype(BF16)
        return carry

    def relay_p(w, keep):
        for t in range(32):
            stage[pl.ds(t * 32, FB), :] = praw[w, :, pl.ds(t * 128, 128)].astype(F32)

        def one_block(b, carry):
            one = stage[pl.ds(b, 32, stride=32), :]
            turn = pltpu.roll(one, BS, 1)
            top = jnp.where(low, one, turn)
            bottom = jnp.where(low, turn, one)
            if keep:
                qperm[pl.ds(pl.multiple_of(b * BS, BS), 32), :] = top
                qperm[pl.ds(pl.multiple_of(b * BS + 32, 32), 32), :] = bottom
            nat[pl.ds(0, 32, stride=2), :] = top
            nat[pl.ds(1, 32, stride=2), :] = bottom
            window[w * FB + b] = nat[...].astype(BF16)
            return carry

        lax.fori_loop(0, FB, one_block, 0)

    relay_p(1, True)
    wide = lax.broadcasted_iota(jnp.int32, (128, 128), 1) < BS
    tall = lax.broadcasted_iota(jnp.int32, (128, 128), 0) // BS
    for g in range(FB // 2):
        block = jnp.transpose(qperm[pl.ds(g * 128, 128), :])
        member = jnp.where(wide, agg_ref[2 * g], agg_ref[2 * g + 1]) - chip * CB
        for u in range(CB // 2):
            turned[pl.ds(u * 128, 128), pl.ds(g * 128, 128)] = jnp.where(
                member == tall + 2 * u, block, 0.0
            ).astype(BF16)

    for i in range(CHUNKS):
        fetches[i].wait()
        lax.fori_loop(i * per, (i + 1) * per, relay_a, 0)

    pl.semaphore_wait(y_sem, ny - 1)
    for c in x_ring:
        pl.semaphore_signal(x_sem, inc=1, device_id=(c, core), device_id_type=MESH)

    to_partner.wait_recv()
    relay_p(2 * other, False)
    to_beyond.wait_recv()
    relay_p(2 * core, False)

    base = (chip * 2 + core - 1) * FB
    pair_copies = []
    for h in range(2):

        def fine_row(f, carry):
            acc = jnp.zeros((BS, HALF), F32)
            for kk in range(KT):
                rows = []
                for k in range(4 * kk, 4 * kk + 4):
                    if k < KA:
                        block = window[jnp.clip(cols_ref[f, k] - base, 0, 3 * FB - 1)]
                        keep = masks[slots_ref[f, k], :, pl.ds(h * HALF, HALF)]
                        keep = jnp.concatenate([keep] * 4, axis=0)
                        rows.append(jnp.concatenate([block, block], axis=1) * keep)
                    else:
                        rows.append(jnp.zeros((BS, HALF), BF16))
                acc += jnp.dot(
                    left[f, :, pl.ds(kk * 256, 256)],
                    jnp.concatenate(rows, axis=0),
                    preferred_element_type=F32,
                )
            summed[pl.ds(pl.multiple_of(f * BS, BS), BS), pl.ds(h * HALF, HALF)] = acc.astype(BF16)
            return carry

        lax.fori_loop(0, FB, fine_row, 0)
        part[h] = jnp.dot(
            turned[...], summed[:, pl.ds(h * HALF, HALF)], preferred_element_type=F32
        )
        copy = pltpu.make_async_remote_copy(
            src_ref=part.at[h],
            dst_ref=theirs.at[h],
            send_sem=pair_send.at[h],
            recv_sem=pair_recv.at[h],
            device_id=(chip, other),
            device_id_type=MESH,
        )
        copy.start()
        pair_copies.append(copy)

    pl.semaphore_wait(x_sem, nx - 1)
    for copy in pair_copies:
        copy.wait()
    whole = jnp.concatenate(
        [(part[h] + theirs[h]).astype(BF16) for h in range(2)], axis=1
    )
    n = min(256, half * 16)
    group = (lax.broadcasted_iota(jnp.int32, (n, 128), 0) // MOST) % 4
    for i in range(half * 16 // n):
        placed = jnp.dot(onehot[pl.ds(i * n, n), :], whole, preferred_element_type=F32)
        value = placed[:, 384:512]
        for b in range(3):
            value = jnp.where(group == b, placed[:, b * 128 : (b + 1) * 128], value)
        for j in range(n // 16):
            outbox[i * (n // 16) + j] = value[j * 16 : (j + 1) * 16].astype(BF16)

    mine = chip % half

    def send(i, sem):
        there = (mine + i) % half
        return pltpu.make_async_remote_copy(
            src_ref=outbox.at[there],
            dst_ref=out_ref.at[chip],
            send_sem=sem,
            recv_sem=out_recv,
            device_id=(side * half + there, core),
            device_id_type=MESH,
        )

    def send_loop(i, carry):
        send(i, out_send).start()
        return carry

    lax.fori_loop(1, half, send_loop, 0)

    @pl.when(core == 0)
    def _():
        pltpu.make_async_copy(outbox.at[mine], out_ref.at[chip], out_recv).start()

    @pl.when(core == 1)
    def _():
        send(0, one_send).start()

    arrived = out_ref.at[pl.ds(side * half, half)]
    pltpu.make_async_copy(arrived, arrived, out_recv).wait()
    forward = pltpu.make_async_remote_copy(
        src_ref=arrived,
        dst_ref=arrived,
        send_sem=fwd_send,
        recv_sem=fwd_recv,
        device_id=(chip, other),
        device_id_type=MESH,
    )
    forward.start()
    sent = outbox.at[pl.ds(0, half - 1)]
    pltpu.make_async_copy(sent, sent, out_send).wait()

    @pl.when(core == 1)
    def _():
        send(0, one_send).wait_send()

    to_partner.wait_send()
    to_beyond.wait_send()
    forward.wait()


def shards(dims, a_blocks, a_cols, slots, prolong, aggregate, owner):
    chips = dims[0] * dims[1] * dims[2]
    half = chips // 2
    anywhere = pl.BlockSpec(memory_space=pl.ANY)
    vmem = pl.BlockSpec(memory_space=pltpu.VMEM)
    smem = pl.BlockSpec(memory_space=pltpu.SMEM)
    dma = pltpu.SemaphoreType.DMA
    arrived = pl.pallas_call(
        functools.partial(kernel, dims),
        out_shape=jax.ShapeDtypeStruct((chips, 16, 128), BF16),
        in_specs=[anywhere, smem, smem, anywhere, smem, vmem],
        out_specs=vmem,
        scratch_shapes=[
            pltpu.VMEM((FB, KA, BS * BS), BF16),
            pltpu.VMEM((3, FB, BS * BS), BF16),
            pltpu.VMEM((32 * 32, 128), F32),
            pltpu.VMEM((BS, 128), F32),
            pltpu.VMEM((FB, BS, KT * 256), BF16),
            pltpu.VMEM((3 * FB, BS, 128), BF16),
            pltpu.VMEM((KC, 16, COLS), BF16),
            pltpu.VMEM((FB * BS, 128), F32),
            pltpu.VMEM((ROWS, FB * BS), BF16),
            pltpu.VMEM((FB * BS, COLS), BF16),
            pltpu.VMEM((half * 16, ROWS), BF16),
            pltpu.VMEM((2, ROWS, HALF), F32),
            pltpu.VMEM((2, ROWS, HALF), F32),
            pltpu.VMEM((half, 16, 128), BF16),
            dma((CHUNKS,)),
            dma,
            dma((2,)),
            dma((2,)),
            dma((2,)),
            dma((2,)),
            dma,
            dma,
            dma,
            dma,
            dma,
            pltpu.SemaphoreType.REGULAR,
            pltpu.SemaphoreType.REGULAR,
        ],
        compiler_params=pltpu.CompilerParams(
            collective_id=0, has_side_effects=True, vmem_limit_bytes=48 * 1024 * 1024
        ),
    )(a_blocks, a_cols, slots, prolong, aggregate, owner)
    rows = arrived.reshape(chips, 4, MOST, 128).astype(F32)
    return jnp.transpose(rows, (0, 2, 1, 3)).reshape(1, chips, MOST, COLS)


def solution(mesh):
    in_specs = (
        P(("rows", "pair"), None, None),
        P(("rows", "pair"), None),
        P(("rows", "pair"), None),
        P(("rows", "pair"), None),
        P(("rows", "pair")),
        P("rows", None),
    )
    out_specs = P("rows", None, None, None)
    return jax.shard_map(
        functools.partial(shards, DIMS),
        mesh=mesh,
        in_specs=in_specs,
        out_specs=out_specs,
        check_vma=False,
    )
```

```python
import functools

import jax
import jax.numpy as jnp
from jax import lax
from jax.experimental import pallas as pl
from jax.experimental.pallas import tpu as pltpu
from jax.sharding import PartitionSpec as P

BS = 64
KA = 27
KC = 8
FB = 24
CB = 4
MOST = 4
ROWS = CB * BS
COLS = KC * BS
HALF = COLS // 2
KT = 7
DIMS = (8, 4, 4)
MESH = pl.DeviceIdType.MESH
BF16 = jnp.bfloat16
F32 = jnp.float32


def fold_blocks(one, two, low):
    top = jnp.where(low, one, pltpu.roll(two, BS, 1))
    bottom = jnp.where(low, pltpu.roll(one, BS, 1), two)
    return top, bottom


def low_lanes():
    return lax.broadcasted_iota(jnp.int32, (32, 128), 1) < BS


def relay_a(g, a_ref, stage, left):
    low = low_lanes()
    for half in range(2):
        for t in range(32):
            stage[half, pl.ds(t * 32, FB), :] = a_ref[
                jnp.minimum(2 * g + half, KA - 1), :, pl.ds(t * 128, 128)
            ].astype(F32)
    column = pl.ds(pl.multiple_of(g * 128, 128), 128)
    for f in range(FB):
        one = stage[0, pl.ds(f, 32, stride=32), :]
        two = stage[1, pl.ds(f, 32, stride=32), :]
        top, bottom = fold_blocks(one, two, low)
        left[f, pl.ds(0, 32), column] = top.astype(BF16)
        left[f, pl.ds(32, 32), column] = bottom.astype(BF16)


def relay_p(w, keep, praw, stage, nat, window, qperm):
    low = low_lanes()
    for t in range(32):
        stage[0, pl.ds(t * 32, FB), :] = praw[w, :, pl.ds(t * 128, 128)].astype(F32)
    for b in range(FB):
        one = stage[0, pl.ds(b, 32, stride=32), :]
        top, bottom = fold_blocks(one, one, low)
        if keep:
            qperm[pl.ds(b * BS, 32), :] = top
            qperm[pl.ds(b * BS + 32, 32), :] = bottom
        nat[b % 4, pl.ds(0, 32, stride=2), :] = top
        nat[b % 4, pl.ds(1, 32, stride=2), :] = bottom
        window[w * FB + b] = nat[b % 4].astype(BF16)


def fill_masks(masks):
    column_slot = lax.broadcasted_iota(jnp.int32, (16, COLS), 1) // BS
    for s in range(KC):
        masks[s] = jnp.where(column_slot == s, 1.0, 0.0).astype(BF16)


def fill_onehot(side, half, owner_ref, onehot):
    owner_row = jnp.broadcast_to(owner_ref[...].astype(F32), (128, ROWS))
    owners = jnp.transpose(owner_row)
    target = jnp.where(
        owners == lax.broadcasted_iota(jnp.int32, (ROWS, 128), 1).astype(F32), 1.0, 0.0
    )
    earlier = jnp.where(
        lax.broadcasted_iota(jnp.int32, (ROWS, ROWS), 0)
        > lax.broadcasted_iota(jnp.int32, (ROWS, ROWS), 1),
        1.0,
        0.0,
    ).astype(BF16)
    before = jnp.dot(earlier, target.astype(BF16), preferred_element_type=F32)
    rank = jnp.sum(before * target, axis=1, keepdims=True)
    key_row = jnp.transpose(owners * MOST + rank)[0:1, :]
    n = min(256, half * 16)
    row_id = lax.broadcasted_iota(jnp.int32, (n, ROWS), 0)
    for i in range(half * 16 // n):
        rid = row_id + i * n
        code = (side * half + rid // 16) * MOST + rid % MOST
        onehot[pl.ds(i * n, n), :] = jnp.where(code.astype(F32) == key_row, 1.0, 0.0).astype(BF16)


def fill_turned(chip, agg_ref, qperm, turned):
    wide = lax.broadcasted_iota(jnp.int32, (128, 128), 1) < BS
    tall = lax.broadcasted_iota(jnp.int32, (128, 128), 0) // BS
    for g in range(FB // 2):
        block = jnp.transpose(qperm[pl.ds(g * 128, 128), :])
        member = jnp.where(wide, agg_ref[2 * g], agg_ref[2 * g + 1]) - chip * CB
        for u in range(CB // 2):
            turned[pl.ds(u * 128, 128), pl.ds(g * 128, 128)] = jnp.where(
                member == tall + 2 * u, block, 0.0
            ).astype(BF16)


def fine_row(f, h, base, cols_ref, slots_ref, left, window, masks, summed):
    acc = jnp.zeros((BS, HALF), F32)
    for kk in range(KT):
        rows = []
        for k in range(4 * kk, 4 * kk + 4):
            if k < KA:
                block = window[jnp.clip(cols_ref[f, k] - base, 0, 3 * FB - 1)]
                keep = masks[slots_ref[f, k], :, pl.ds(h * HALF, HALF)]
                keep = jnp.concatenate([keep] * 4, axis=0)
                rows.append(jnp.concatenate([block, block], axis=1) * keep)
            else:
                rows.append(jnp.zeros((BS, HALF), BF16))
        acc += jnp.dot(
            left[f, :, pl.ds(kk * 256, 256)],
            jnp.concatenate(rows, axis=0),
            preferred_element_type=F32,
        )
    summed[pl.ds(pl.multiple_of(f * BS, BS), BS), pl.ds(h * HALF, HALF)] = acc.astype(BF16)


def place(half, onehot, part, theirs, outbox):
    whole = jnp.concatenate([(part[h] + theirs[h]).astype(BF16) for h in range(2)], axis=1)
    n = min(256, half * 16)
    group = (lax.broadcasted_iota(jnp.int32, (n, 128), 0) // MOST) % 4
    for i in range(half * 16 // n):
        placed = jnp.dot(onehot[pl.ds(i * n, n), :], whole, preferred_element_type=F32)
        value = placed[:, 384:512]
        for b in range(3):
            value = jnp.where(group == b, placed[:, b * 128 : (b + 1) * 128], value)
        for j in range(n // 16):
            outbox[i * (n // 16) + j] = value[j * 16 : (j + 1) * 16].astype(BF16)


def kernel(
    dims,
    a_hbm,
    cols_ref,
    slots_ref,
    prolong_hbm,
    agg_ref,
    owner_ref,
    out_ref,
    a_ref,
    praw,
    stage,
    nat,
    left,
    window,
    masks,
    qperm,
    turned,
    summed,
    onehot,
    part,
    theirs,
    outbox,
    a_sem,
    p_sem,
    near_send,
    near_recv,
    pair_send,
    pair_recv,
    out_send,
    one_send,
    out_recv,
    fwd_send,
    fwd_recv,
    y_sem,
    x_sem,
):
    nz, nx, ny = dims
    chips = nz * nx * ny
    half = chips // 2
    chip = lax.axis_index("rows")
    core = lax.axis_index("pair")
    other = 1 - core
    z, x, y = chip // (nx * ny), (chip // ny) % nx, chip % ny
    beyond = (chip + chips - 1 + 2 * core) % chips

    fetches = []
    for i in range(KT):
        span = pl.ds(4 * i, min(4, KA - 4 * i))
        fetches.append(pltpu.make_async_copy(a_hbm.at[span], a_ref.at[span], a_sem.at[i]))
    own = pltpu.make_async_copy(prolong_hbm, praw.at[1], p_sem)
    own.start()
    for fetch in fetches:
        fetch.start()

    y_ring = [(z * nx + x) * ny + (y + i) % ny for i in range(1, ny)]
    x_ring = [(z * nx + (x + i) % nx) * ny + y for i in range(1, nx)]
    z_ring = [(((z + i) % nz) * nx + x) * ny + y for i in range(1, nz)]
    barrier = pltpu.get_barrier_semaphore()
    met = [(chip, other), (beyond, other)] + [(c, core) for c in y_ring + x_ring + z_ring]
    for device in met:
        pl.semaphore_signal(barrier, inc=1, device_id=device, device_id_type=MESH)
    own.wait()
    pl.semaphore_wait(barrier, len(met))

    to_partner = pltpu.make_async_remote_copy(
        src_ref=praw.at[1],
        dst_ref=praw.at[2 * core],
        send_sem=near_send.at[0],
        recv_sem=near_recv.at[0],
        device_id=(chip, other),
        device_id_type=MESH,
    )
    to_beyond = pltpu.make_async_remote_copy(
        src_ref=praw.at[1],
        dst_ref=praw.at[2 * other],
        send_sem=near_send.at[1],
        recv_sem=near_recv.at[1],
        device_id=(beyond, other),
        device_id_type=MESH,
    )
    to_beyond.start()
    to_partner.start()
    for c in y_ring:
        pl.semaphore_signal(y_sem, inc=1, device_id=(c, core), device_id_type=MESH)

    side = (chip // half + core) % 2
    fill_masks(masks)
    fill_onehot(side, half, owner_ref, onehot)
    relay_p(1, True, praw, stage, nat, window, qperm)
    fill_turned(chip, agg_ref, qperm, turned)

    for i in range(KT):
        fetches[i].wait()

        def relay(g, carry):
            relay_a(g, a_ref, stage, left)
            return carry

        lax.fori_loop(2 * i, 2 * i + 2, relay, 0)

    pl.semaphore_wait(y_sem, ny - 1)
    for c in x_ring:
        pl.semaphore_signal(x_sem, inc=1, device_id=(c, core), device_id_type=MESH)

    to_partner.wait_recv()
    relay_p(2 * other, False, praw, stage, nat, window, qperm)
    to_beyond.wait_recv()
    relay_p(2 * core, False, praw, stage, nat, window, qperm)

    base = (chip * 2 + core - 1) * FB
    pair_copies = []
    for h in range(2):

        def row(f, carry):
            fine_row(f, h, base, cols_ref, slots_ref, left, window, masks, summed)
            return carry

        lax.fori_loop(0, FB, row, 0)
        part[h] = jnp.dot(
            turned[...], summed[:, pl.ds(h * HALF, HALF)], preferred_element_type=F32
        )
        copy = pltpu.make_async_remote_copy(
            src_ref=part.at[h],
            dst_ref=theirs.at[h],
            send_sem=pair_send.at[h],
            recv_sem=pair_recv.at[h],
            device_id=(chip, other),
            device_id_type=MESH,
        )
        copy.start()
        pair_copies.append(copy)

    pl.semaphore_wait(x_sem, nx - 1)
    for copy in pair_copies:
        copy.wait()
    place(half, onehot, part, theirs, outbox)

    mine = chip % half

    def send(i, sem):
        there = (mine + i) % half
        return pltpu.make_async_remote_copy(
            src_ref=outbox.at[there],
            dst_ref=out_ref.at[chip],
            send_sem=sem,
            recv_sem=out_recv,
            device_id=(side * half + there, core),
            device_id_type=MESH,
        )

    def send_loop(i, carry):
        send(i, out_send).start()
        return carry

    lax.fori_loop(1, half, send_loop, 0)

    @pl.when(core == 0)
    def _():
        pltpu.make_async_copy(outbox.at[mine], out_ref.at[chip], out_recv).start()

    @pl.when(core == 1)
    def _():
        send(0, one_send).start()

    arrived = out_ref.at[pl.ds(side * half, half)]
    pltpu.make_async_copy(arrived, arrived, out_recv).wait()
    forward = pltpu.make_async_remote_copy(
        src_ref=arrived,
        dst_ref=arrived,
        send_sem=fwd_send,
        recv_sem=fwd_recv,
        device_id=(chip, other),
        device_id_type=MESH,
    )
    forward.start()
    sent = outbox.at[pl.ds(0, half - 1)]
    pltpu.make_async_copy(sent, sent, out_send).wait()

    @pl.when(core == 1)
    def _():
        send(0, one_send).wait_send()

    to_partner.wait_send()
    to_beyond.wait_send()
    forward.wait()


def shards(dims, a_blocks, a_cols, slots, prolong, aggregate, owner):
    chips = dims[0] * dims[1] * dims[2]
    half = chips // 2
    anywhere = pl.BlockSpec(memory_space=pl.ANY)
    vmem = pl.BlockSpec(memory_space=pltpu.VMEM)
    smem = pl.BlockSpec(memory_space=pltpu.SMEM)
    dma = pltpu.SemaphoreType.DMA
    arrived = pl.pallas_call(
        functools.partial(kernel, dims),
        out_shape=jax.ShapeDtypeStruct((chips, 16, 128), BF16),
        in_specs=[anywhere, smem, smem, anywhere, smem, vmem],
        out_specs=vmem,
        scratch_shapes=[
            pltpu.VMEM((KA, FB, BS * BS), BF16),
            pltpu.VMEM((3, FB, BS * BS), BF16),
            pltpu.VMEM((2, 32 * 32, 128), F32),
            pltpu.VMEM((4, BS, 128), F32),
            pltpu.VMEM((FB, BS, KT * 256), BF16),
            pltpu.VMEM((3 * FB, BS, 128), BF16),
            pltpu.VMEM((KC, 16, COLS), BF16),
            pltpu.VMEM((FB * BS, 128), F32),
            pltpu.VMEM((ROWS, FB * BS), BF16),
            pltpu.VMEM((FB * BS, COLS), BF16),
            pltpu.VMEM((half * 16, ROWS), BF16),
            pltpu.VMEM((2, ROWS, HALF), F32),
            pltpu.VMEM((2, ROWS, HALF), F32),
            pltpu.VMEM((half, 16, 128), BF16),
            dma((KT,)),
            dma,
            dma((2,)),
            dma((2,)),
            dma((2,)),
            dma((2,)),
            dma,
            dma,
            dma,
            dma,
            dma,
            pltpu.SemaphoreType.REGULAR,
            pltpu.SemaphoreType.REGULAR,
        ],
        compiler_params=pltpu.CompilerParams(
            collective_id=0, has_side_effects=True, vmem_limit_bytes=48 * 1024 * 1024
        ),
    )(
        jnp.transpose(a_blocks, (1, 0, 2)),
        a_cols,
        slots,
        prolong,
        aggregate,
        owner.reshape(1, ROWS),
    )
    rows = arrived.reshape(chips, 4, MOST, 128).astype(F32)
    return jnp.transpose(rows, (0, 2, 1, 3)).reshape(1, chips, MOST, COLS)


def solution(mesh):
    in_specs = (
        P(("rows", "pair"), None, None),
        P(("rows", "pair"), None),
        P(("rows", "pair"), None),
        P(("rows", "pair"), None),
        P(("rows", "pair")),
        P("rows", None),
    )
    out_specs = P("rows", None, None, None)
    return jax.shard_map(
        functools.partial(shards, DIMS),
        mesh=mesh,
        in_specs=in_specs,
        out_specs=out_specs,
        check_vma=False,
    )
```

```python
import functools

import jax
import jax.numpy as jnp
from jax import lax
from jax.experimental import pallas as pl
from jax.experimental.pallas import tpu as pltpu
from jax.sharding import PartitionSpec as P

BS = 64
KA = 27
KC = 8
FB = 24
CB = 4
MOST = 4
ROWS = CB * BS
COLS = KC * BS
HALF = COLS // 2
KT = 7
SKEW = 25
TOGETHER = 4
DIMS = (8, 4, 4)
MESH = pl.DeviceIdType.MESH
BF16 = jnp.bfloat16
F32 = jnp.float32


def fold_blocks(one, two, low):
    top = jnp.where(low, one, pltpu.roll(two, BS, 1))
    bottom = jnp.where(low, pltpu.roll(one, BS, 1), two)
    return top, bottom


def low_lanes():
    return lax.broadcasted_iota(jnp.int32, (32, 128), 1) < BS


def relay_a(g, a_ref, stage, left):
    low = low_lanes()
    for half in range(2):
        for t in range(32):
            stage[half, pl.ds(t * SKEW, FB), :] = a_ref[
                jnp.minimum(2 * g + half, KA - 1), :, pl.ds(t * 128, 128)
            ].astype(F32)
    column = pl.ds(pl.multiple_of(g * 128, 128), 128)
    for f in range(FB):
        one = stage[0, pl.ds(f, 32, stride=SKEW), :]
        two = stage[1, pl.ds(f, 32, stride=SKEW), :]
        top, bottom = fold_blocks(one, two, low)
        left[f, pl.ds(0, 32), column] = top.astype(BF16)
        left[f, pl.ds(32, 32), column] = bottom.astype(BF16)


def relay_p(w, keep, praw, stage, nat, window, qperm):
    low = low_lanes()
    for t in range(32):
        stage[0, pl.ds(t * SKEW, FB), :] = praw[w, :, pl.ds(t * 128, 128)].astype(F32)
    for b in range(FB):
        one = stage[0, pl.ds(b, 32, stride=SKEW), :]
        top, bottom = fold_blocks(one, one, low)
        if keep:
            qperm[pl.ds(b * BS, 32), :] = top
            qperm[pl.ds(b * BS + 32, 32), :] = bottom
        nat[b % 4, pl.ds(0, 32, stride=2), :] = top
        nat[b % 4, pl.ds(1, 32, stride=2), :] = bottom
        window[w * FB + b] = nat[b % 4].astype(BF16)


def fill_masks(slot_mask, side_mask):
    column_slot = lax.broadcasted_iota(jnp.int32, (16, HALF), 1) // BS
    first = lax.broadcasted_iota(jnp.int32, (16, 128), 1) < BS
    for s in range(KC):
        slot_mask[s] = jnp.where(column_slot == s % 4, 1.0, 0.0).astype(BF16)
        for t in range(KC):
            below = jnp.where(first, 1.0 - s // 4, 1.0 - t // 4)
            side_mask[KC * s + t, :, 0:128] = below.astype(BF16)
            side_mask[KC * s + t, :, 128:256] = (1.0 - below).astype(BF16)


def fill_onehot(side, half, owner_ref, onehot):
    owner_row = jnp.broadcast_to(owner_ref[...].astype(F32), (128, ROWS))
    owners = jnp.transpose(owner_row)
    target = jnp.where(
        owners == lax.broadcasted_iota(jnp.int32, (ROWS, 128), 1).astype(F32), 1.0, 0.0
    )
    earlier = jnp.where(
        lax.broadcasted_iota(jnp.int32, (ROWS, ROWS), 0)
        > lax.broadcasted_iota(jnp.int32, (ROWS, ROWS), 1),
        1.0,
        0.0,
    ).astype(BF16)
    before = jnp.dot(earlier, target.astype(BF16), preferred_element_type=F32)
    rank = jnp.sum(before * target, axis=1, keepdims=True)
    key_row = jnp.transpose(owners * MOST + rank)[0:1, :]
    n = min(256, half * 16)
    row_id = lax.broadcasted_iota(jnp.int32, (n, ROWS), 0)
    for i in range(half * 16 // n):
        rid = row_id + i * n
        code = (side * half + rid // 16) * MOST + rid % MOST
        onehot[pl.ds(i * n, n), :] = jnp.where(code.astype(F32) == key_row, 1.0, 0.0).astype(BF16)


def fill_turned(chip, agg_ref, qperm, turned):
    wide = lax.broadcasted_iota(jnp.int32, (128, 128), 1) < BS
    tall = lax.broadcasted_iota(jnp.int32, (128, 128), 0) // BS
    for g in range(FB // 2):
        block = jnp.transpose(qperm[pl.ds(g * 128, 128), :])
        member = jnp.where(wide, agg_ref[2 * g], agg_ref[2 * g + 1]) - chip * CB
        for u in range(CB // 2):
            turned[pl.ds(u * 128, 128), pl.ds(g * 128, 128)] = jnp.where(
                member == tall + 2 * u, block, 0.0
            ).astype(BF16)


def tall(mask):
    return jnp.concatenate([mask] * (BS // 16), axis=0)


def positions(f, kk, base, cols_ref, slots_ref, left, window, slot_mask, side_mask):
    blocks, low, high = [], [], []
    for k in (4 * kk, 4 * kk + 2):
        slots = [slots_ref[f, min(k + i, KA - 1)] for i in range(2)]
        for i in range(2):
            if k + i < KA:
                block = window[jnp.clip(cols_ref[f, k + i] - base, 0, 3 * FB - 1)]
                keep = tall(slot_mask[slots[i]])
                blocks.append(jnp.concatenate([block, block], axis=1) * keep)
            else:
                blocks.append(jnp.zeros((BS, HALF), BF16))
        pair = left[f, :, pl.ds(k * BS, 128)]
        keep = side_mask[slots[0] * KC + slots[1]]
        low.append(pair * tall(keep[:, 0:128]))
        high.append(pair * tall(keep[:, 128:256]))
    rows = [jnp.concatenate(low, axis=1), jnp.concatenate(high, axis=1)]
    return jnp.dot(
        jnp.concatenate(rows, axis=0),
        jnp.concatenate(blocks, axis=0),
        preferred_element_type=F32,
    )


def fine_rows(g, base, cols_ref, slots_ref, left, window, slot_mask, side_mask, summed):
    total = [None] * TOGETHER
    for kk in range(KT):
        for i in range(TOGETHER):
            f = g * TOGETHER + i
            term = positions(
                f, kk, base, cols_ref, slots_ref, left, window, slot_mask, side_mask
            )
            total[i] = term if kk == 0 else total[i] + term
    for i in range(TOGETHER):
        rows = pl.ds(pl.multiple_of((g * TOGETHER + i) * BS, BS), BS)
        summed[rows, 0:HALF] = total[i][0:BS].astype(BF16)
        summed[rows, HALF:COLS] = total[i][BS:].astype(BF16)


def place(half, onehot, part, theirs, outbox):
    whole = jnp.concatenate([(part[h] + theirs[h]).astype(BF16) for h in range(2)], axis=1)
    n = min(256, half * 16)
    group = (lax.broadcasted_iota(jnp.int32, (n, 128), 0) // MOST) % 4
    for i in range(half * 16 // n):
        placed = jnp.dot(onehot[pl.ds(i * n, n), :], whole, preferred_element_type=F32)
        value = placed[:, 384:512]
        for b in range(3):
            value = jnp.where(group == b, placed[:, b * 128 : (b + 1) * 128], value)
        for j in range(n // 16):
            outbox[i * (n // 16) + j] = value[j * 16 : (j + 1) * 16].astype(BF16)


def kernel(
    dims,
    a_hbm,
    cols_hbm,
    slots_hbm,
    prolong_hbm,
    agg_hbm,
    owner_hbm,
    out_ref,
    cols_ref,
    slots_ref,
    agg_ref,
    owner_ref,
    a_ref,
    praw,
    stage,
    nat,
    left,
    window,
    slot_mask,
    side_mask,
    qperm,
    turned,
    summed,
    onehot,
    part,
    theirs,
    outbox,
    a_sem,
    p_sem,
    small_sem,
    near_send,
    near_recv,
    pair_send,
    pair_recv,
    out_send,
    one_send,
    out_recv,
    fwd_send,
    fwd_recv,
    y_sem,
    x_sem,
):
    nz, nx, ny = dims
    chips = nz * nx * ny
    half = chips // 2
    chip = lax.axis_index("rows")
    core = lax.axis_index("pair")
    other = 1 - core
    z, x, y = chip // (nx * ny), (chip // ny) % nx, chip % ny
    beyond = (chip + chips - 1 + 2 * core) % chips

    fetches = []
    for i in range(KT):
        span = pl.ds(4 * i, min(4, KA - 4 * i))
        fetches.append(pltpu.make_async_copy(a_hbm.at[span], a_ref.at[span], a_sem.at[i]))
    own = pltpu.make_async_copy(prolong_hbm, praw.at[1], p_sem)
    own.start()
    small = [
        pltpu.make_async_copy(src, dst, small_sem.at[i])
        for i, (src, dst) in enumerate(
            [
                (owner_hbm, owner_ref),
                (agg_hbm, agg_ref),
                (cols_hbm, cols_ref),
                (slots_hbm, slots_ref),
            ]
        )
    ]
    for copy in small:
        copy.start()
    for fetch in fetches:
        fetch.start()

    y_ring = [(z * nx + x) * ny + (y + i) % ny for i in range(1, ny)]
    x_ring = [(z * nx + (x + i) % nx) * ny + y for i in range(1, nx)]
    z_ring = [(((z + i) % nz) * nx + x) * ny + y for i in range(1, nz)]
    barrier = pltpu.get_barrier_semaphore()
    met = [(chip, other), (beyond, other)] + [(c, core) for c in y_ring + x_ring + z_ring]
    for device in met:
        pl.semaphore_signal(barrier, inc=1, device_id=device, device_id_type=MESH)
    own.wait()
    pl.semaphore_wait(barrier, len(met))

    to_partner = pltpu.make_async_remote_copy(
        src_ref=praw.at[1],
        dst_ref=praw.at[2 * core],
        send_sem=near_send.at[0],
        recv_sem=near_recv.at[0],
        device_id=(chip, other),
        device_id_type=MESH,
    )
    to_beyond = pltpu.make_async_remote_copy(
        src_ref=praw.at[1],
        dst_ref=praw.at[2 * other],
        send_sem=near_send.at[1],
        recv_sem=near_recv.at[1],
        device_id=(beyond, other),
        device_id_type=MESH,
    )
    to_beyond.start()
    to_partner.start()
    for c in y_ring:
        pl.semaphore_signal(y_sem, inc=1, device_id=(c, core), device_id_type=MESH)

    side = (chip // half + core) % 2
    fill_masks(slot_mask, side_mask)
    small[0].wait()
    fill_onehot(side, half, owner_ref, onehot)
    relay_p(1, True, praw, stage, nat, window, qperm)
    small[1].wait()
    fill_turned(chip, agg_ref, qperm, turned)

    for i in range(KT):
        fetches[i].wait()

        def relay(g, carry):
            relay_a(g, a_ref, stage, left)
            return carry

        lax.fori_loop(2 * i, 2 * i + 2, relay, 0)

    pl.semaphore_wait(y_sem, ny - 1)
    for c in x_ring:
        pl.semaphore_signal(x_sem, inc=1, device_id=(c, core), device_id_type=MESH)

    to_partner.wait_recv()
    relay_p(2 * other, False, praw, stage, nat, window, qperm)
    to_beyond.wait_recv()
    relay_p(2 * core, False, praw, stage, nat, window, qperm)

    small[2].wait()
    small[3].wait()
    base = (chip * 2 + core - 1) * FB

    def rows_step(g, carry):
        fine_rows(g, base, cols_ref, slots_ref, left, window, slot_mask, side_mask, summed)
        return carry

    lax.fori_loop(0, FB // TOGETHER, rows_step, 0)
    pair_copies = []
    for h in range(2):
        part[h] = jnp.dot(
            turned[...], summed[:, pl.ds(h * HALF, HALF)], preferred_element_type=F32
        )
        copy = pltpu.make_async_remote_copy(
            src_ref=part.at[h],
            dst_ref=theirs.at[h],
            send_sem=pair_send.at[h],
            recv_sem=pair_recv.at[h],
            device_id=(chip, other),
            device_id_type=MESH,
        )
        copy.start()
        pair_copies.append(copy)

    pl.semaphore_wait(x_sem, nx - 1)
    for copy in pair_copies:
        copy.wait()
    place(half, onehot, part, theirs, outbox)

    mine = chip % half

    def send(i, sem):
        there = (mine + i) % half
        return pltpu.make_async_remote_copy(
            src_ref=outbox.at[there],
            dst_ref=out_ref.at[chip],
            send_sem=sem,
            recv_sem=out_recv,
            device_id=(side * half + there, core),
            device_id_type=MESH,
        )

    def send_loop(i, carry):
        send(i, out_send).start()
        return carry

    lax.fori_loop(1, half, send_loop, 0)

    @pl.when(core == 0)
    def _():
        pltpu.make_async_copy(outbox.at[mine], out_ref.at[chip], out_recv).start()

    @pl.when(core == 1)
    def _():
        send(0, one_send).start()

    arrived = out_ref.at[pl.ds(side * half, half)]
    pltpu.make_async_copy(arrived, arrived, out_recv).wait()
    forward = pltpu.make_async_remote_copy(
        src_ref=arrived,
        dst_ref=arrived,
        send_sem=fwd_send,
        recv_sem=fwd_recv,
        device_id=(chip, other),
        device_id_type=MESH,
    )
    forward.start()
    sent = outbox.at[pl.ds(0, half - 1)]
    pltpu.make_async_copy(sent, sent, out_send).wait()

    @pl.when(core == 1)
    def _():
        send(0, one_send).wait_send()

    to_partner.wait_send()
    to_beyond.wait_send()
    forward.wait()


def shards(dims, a_blocks, a_cols, slots, prolong, aggregate, owner):
    chips = dims[0] * dims[1] * dims[2]
    half = chips // 2
    hbm = pl.BlockSpec(memory_space=pltpu.HBM)
    vmem = pl.BlockSpec(memory_space=pltpu.VMEM)
    dma = pltpu.SemaphoreType.DMA
    arrived = pl.pallas_call(
        functools.partial(kernel, dims),
        out_shape=jax.ShapeDtypeStruct((chips, 16, 128), BF16),
        in_specs=[hbm] * 6,
        out_specs=vmem,
        scratch_shapes=[
            pltpu.SMEM((FB, KA), jnp.int32),
            pltpu.SMEM((FB, KA), jnp.int32),
            pltpu.SMEM((FB,), jnp.int32),
            pltpu.VMEM((1, ROWS), jnp.int32),
            pltpu.VMEM((KA, FB, BS * BS), BF16),
            pltpu.VMEM((3, FB, BS * BS), BF16),
            pltpu.VMEM((2, 32 * 32, 128), F32),
            pltpu.VMEM((4, BS, 128), F32),
            pltpu.VMEM((FB, BS, KT * 256), BF16),
            pltpu.VMEM((3 * FB, BS, 128), BF16),
            pltpu.VMEM((KC, 16, HALF), BF16),
            pltpu.VMEM((KC * KC, 16, HALF), BF16),
            pltpu.VMEM((FB * BS, 128), F32),
            pltpu.VMEM((ROWS, FB * BS), BF16),
            pltpu.VMEM((FB * BS, COLS), BF16),
            pltpu.VMEM((half * 16, ROWS), BF16),
            pltpu.VMEM((2, ROWS, HALF), F32),
            pltpu.VMEM((2, ROWS, HALF), F32),
            pltpu.VMEM((half, 16, 128), BF16),
            dma((KT,)),
            dma,
            dma((4,)),
            dma((2,)),
            dma((2,)),
            dma((2,)),
            dma((2,)),
            dma,
            dma,
            dma,
            dma,
            dma,
            pltpu.SemaphoreType.REGULAR,
            pltpu.SemaphoreType.REGULAR,
        ],
        compiler_params=pltpu.CompilerParams(
            collective_id=0, has_side_effects=True, vmem_limit_bytes=60 * 1024 * 1024
        ),
    )(
        jnp.transpose(a_blocks, (1, 0, 2)),
        a_cols,
        slots,
        prolong,
        aggregate,
        owner.reshape(1, ROWS),
    )
    rows = arrived.reshape(chips, 4, MOST, 128).astype(F32)
    return jnp.transpose(rows, (0, 2, 1, 3)).reshape(1, chips, MOST, COLS)


def solution(mesh):
    in_specs = (
        P(("rows", "pair"), None, None),
        P(("rows", "pair"), None),
        P(("rows", "pair"), None),
        P(("rows", "pair"), None),
        P(("rows", "pair")),
        P("rows", None),
    )
    out_specs = P("rows", None, None, None)
    return jax.shard_map(
        functools.partial(shards, DIMS),
        mesh=mesh,
        in_specs=in_specs,
        out_specs=out_specs,
        check_vma=False,
    )
```

```python
import functools

import jax
import jax.numpy as jnp
from jax import lax
from jax.experimental import pallas as pl
from jax.experimental.pallas import tpu as pltpu
from jax.sharding import PartitionSpec as P

BS = 64
KA = 27
KC = 8
FB = 24
CB = 4
MOST = 4
ROWS = CB * BS
COLS = KC * BS
HALF = COLS // 2
KT = 7
SKEW = 25
PIECES = 2
SENDS = 32
TOGETHER = 4
DIMS = (8, 4, 4)
MESH = pl.DeviceIdType.MESH
BF16 = jnp.bfloat16
F32 = jnp.float32


def fold_blocks(one, two, low):
    top = jnp.where(low, one, pltpu.roll(two, BS, 1))
    bottom = jnp.where(low, pltpu.roll(one, BS, 1), two)
    return top, bottom


def low_lanes():
    return lax.broadcasted_iota(jnp.int32, (32, 128), 1) < BS


def relay_a(g, a_ref, stage, left):
    low = low_lanes()
    for half in range(2):
        for t in range(32):
            stage[half, pl.ds(t * SKEW, FB), :] = a_ref[
                jnp.minimum(2 * g + half, KA - 1), :, pl.ds(t * 128, 128)
            ].astype(F32)
    column = pl.ds(pl.multiple_of(g * 128, 128), 128)
    for f in range(FB):
        one = stage[0, pl.ds(f, 32, stride=SKEW), :]
        two = stage[1, pl.ds(f, 32, stride=SKEW), :]
        top, bottom = fold_blocks(one, two, low)
        left[f, pl.ds(0, 32), column] = top.astype(BF16)
        left[f, pl.ds(32, 32), column] = bottom.astype(BF16)


def relay_p(w, keep, praw, stage, nat, window, qperm):
    low = low_lanes()
    for t in range(32):
        stage[0, pl.ds(t * SKEW, FB), :] = praw[w, :, pl.ds(t * 128, 128)].astype(F32)
    for b in range(FB):
        one = stage[0, pl.ds(b, 32, stride=SKEW), :]
        top, bottom = fold_blocks(one, one, low)
        if keep:
            qperm[pl.ds(b * BS, 32), :] = top
            qperm[pl.ds(b * BS + 32, 32), :] = bottom
        nat[b % 4, pl.ds(0, 32, stride=2), :] = top
        nat[b % 4, pl.ds(1, 32, stride=2), :] = bottom
        window[w * FB + b] = nat[b % 4].astype(BF16)


def fill_masks(slot_mask, side_mask):
    column_slot = lax.broadcasted_iota(jnp.int32, (16, HALF), 1) // BS
    first = lax.broadcasted_iota(jnp.int32, (16, 128), 1) < BS
    for s in range(KC):
        slot_mask[s] = jnp.where(column_slot == s % 4, 1.0, 0.0).astype(BF16)
        for t in range(KC):
            below = jnp.where(first, 1.0 - s // 4, 1.0 - t // 4)
            side_mask[KC * s + t, :, 0:128] = below.astype(BF16)
            side_mask[KC * s + t, :, 128:256] = (1.0 - below).astype(BF16)


def spread(i, n):
    return n // 2 + (i + 1) // 2 * (1 - 2 * (i % 2))


def plane_order(dims, z):
    nz, nx, ny = dims
    return [(z + spread(i, nz)) % nz * (nx * ny) for i in range(nz)]


def column_order(i, dims, x, y):
    nz, nx, ny = dims
    return (x + spread(i // ny, nx)) % nx * ny + (y + spread(i % ny, ny)) % ny


def fill_onehot(dims, place_of, owner_ref, onehot):
    nz, nx, ny = dims
    z, x, y = place_of
    owner_row = jnp.broadcast_to(owner_ref[...].astype(F32), (128, ROWS))
    owners = jnp.transpose(owner_row)
    target = jnp.where(
        owners == lax.broadcasted_iota(jnp.int32, (ROWS, 128), 1).astype(F32), 1.0, 0.0
    )
    earlier = jnp.where(
        lax.broadcasted_iota(jnp.int32, (ROWS, ROWS), 0)
        > lax.broadcasted_iota(jnp.int32, (ROWS, ROWS), 1),
        1.0,
        0.0,
    ).astype(BF16)
    before = jnp.dot(earlier, target.astype(BF16), preferred_element_type=F32)
    rank = jnp.sum(before * target, axis=1, keepdims=True)
    key_row = jnp.transpose(owners * MOST + rank)[0:1, :]
    slot = lax.broadcasted_iota(jnp.int32, (16, ROWS), 0) % MOST
    upper = lax.broadcasted_iota(jnp.int32, (16, ROWS), 0) // 8
    planes = plane_order(dims, z)

    def column(i, carry):
        there = column_order(i, dims, x, y)
        for u in range(0, nz, 2):
            code = slot + (planes[u] + there) * MOST + upper * ((planes[u + 1] - planes[u]) * MOST)
            rows = pl.ds(pl.multiple_of((i * nz + u) * 8, 16), 16)
            onehot[rows, :] = jnp.where(code.astype(F32) == key_row, 1.0, 0.0).astype(BF16)
        return carry

    lax.fori_loop(0, nx * ny, column, 0)


def fill_turned(chip, agg_ref, qperm, turned):
    wide = lax.broadcasted_iota(jnp.int32, (128, 128), 1) < BS
    tall = lax.broadcasted_iota(jnp.int32, (128, 128), 0) // BS
    for g in range(FB // 2):
        block = jnp.transpose(qperm[pl.ds(g * 128, 128), :])
        member = jnp.where(wide, agg_ref[2 * g], agg_ref[2 * g + 1]) - chip * CB
        for u in range(CB // 2):
            turned[pl.ds(u * 128, 128), pl.ds(g * 128, 128)] = jnp.where(
                member == tall + 2 * u, block, 0.0
            ).astype(BF16)


def tall(mask):
    return jnp.concatenate([mask] * (BS // 16), axis=0)


def positions(f, kk, base, cols_ref, slots_ref, left, window, slot_mask, side_mask):
    blocks, low, high = [], [], []
    for k in (4 * kk, 4 * kk + 2):
        slots = [slots_ref[f, min(k + i, KA - 1)] for i in range(2)]
        for i in range(2):
            if k + i < KA:
                block = window[jnp.clip(cols_ref[f, k + i] - base, 0, 3 * FB - 1)]
                keep = tall(slot_mask[slots[i]])
                blocks.append(jnp.concatenate([block, block], axis=1) * keep)
            else:
                blocks.append(jnp.zeros((BS, HALF), BF16))
        pair = left[f, :, pl.ds(k * BS, 128)]
        keep = side_mask[slots[0] * KC + slots[1]]
        low.append(pair * tall(keep[:, 0:128]))
        high.append(pair * tall(keep[:, 128:256]))
    rows = [jnp.concatenate(low, axis=1), jnp.concatenate(high, axis=1)]
    return jnp.dot(
        jnp.concatenate(rows, axis=0),
        jnp.concatenate(blocks, axis=0),
        preferred_element_type=F32,
    )


def fine_rows(g, base, cols_ref, slots_ref, left, window, slot_mask, side_mask, summed):
    total = [None] * TOGETHER
    for kk in range(KT):
        for i in range(TOGETHER):
            f = g * TOGETHER + i
            term = positions(
                f, kk, base, cols_ref, slots_ref, left, window, slot_mask, side_mask
            )
            total[i] = term if kk == 0 else total[i] + term
    for i in range(TOGETHER):
        rows = pl.ds(pl.multiple_of((g * TOGETHER + i) * BS, BS), BS)
        summed[rows, 0:HALF] = total[i][0:BS].astype(BF16)
        summed[rows, HALF:COLS] = total[i][BS:].astype(BF16)


def place(i, n, whole, onehot, outbox):
    first = (lax.broadcasted_iota(jnp.int32, (8 * n, 128), 0) // MOST) % 2 == 0
    placed = jnp.dot(onehot[pl.ds(i * 8 * n, 8 * n), :], whole, preferred_element_type=F32)
    value = jnp.where(first, placed[:, 0:128], placed[:, 128:256])
    for j in range(n):
        outbox[i * n + j] = value[j * 8 : (j + 1) * 8].astype(BF16)


def kernel(
    dims,
    a_hbm,
    cols_hbm,
    slots_hbm,
    prolong_hbm,
    agg_hbm,
    owner_hbm,
    out_ref,
    cols_ref,
    slots_ref,
    agg_ref,
    owner_ref,
    a_ref,
    praw,
    stage,
    nat,
    left,
    window,
    slot_mask,
    side_mask,
    qperm,
    turned,
    summed,
    onehot,
    part,
    theirs,
    outbox,
    a_sem,
    p_sem,
    small_sem,
    near_send,
    near_recv,
    pair_send,
    pair_recv,
    out_send,
    out_recv,
    fwd_send,
    fwd_recv,
    y_sem,
    x_sem,
):
    nz, nx, ny = dims
    chips = nz * nx * ny
    plane = nx * ny
    chip = lax.axis_index("rows")
    core = lax.axis_index("pair")
    other = 1 - core
    z, x, y = chip // (nx * ny), (chip // ny) % nx, chip % ny
    beyond = (chip + chips - 1 + 2 * core) % chips

    fetches = []
    for i in range(KT):
        span = pl.ds(4 * i, min(4, KA - 4 * i))
        fetches.append(pltpu.make_async_copy(a_hbm.at[span], a_ref.at[span], a_sem.at[i]))
    own = pltpu.make_async_copy(prolong_hbm, praw.at[1], p_sem)
    own.start()
    small = [
        pltpu.make_async_copy(src, dst, small_sem.at[i])
        for i, (src, dst) in enumerate(
            [
                (owner_hbm, owner_ref),
                (agg_hbm, agg_ref),
                (cols_hbm, cols_ref),
                (slots_hbm, slots_ref),
            ]
        )
    ]
    for copy in small:
        copy.start()
    for fetch in fetches:
        fetch.start()

    y_ring = [(z * nx + x) * ny + (y + i) % ny for i in range(1, ny)]
    x_ring = [(z * nx + (x + i) % nx) * ny + y for i in range(1, nx)]
    z_ring = [(((z + i) % nz) * nx + x) * ny + y for i in range(1, nz)]
    barrier = pltpu.get_barrier_semaphore()
    met = [(chip, other), (beyond, other)] + [(c, core) for c in y_ring + x_ring + z_ring]
    for device in met:
        pl.semaphore_signal(barrier, inc=1, device_id=device, device_id_type=MESH)
    pl.semaphore_wait(barrier, len(met))

    to_partner = pltpu.make_async_remote_copy(
        src_ref=prolong_hbm,
        dst_ref=praw.at[2 * core],
        send_sem=near_send.at[0],
        recv_sem=near_recv.at[0],
        device_id=(chip, other),
        device_id_type=MESH,
    )
    to_beyond = pltpu.make_async_remote_copy(
        src_ref=prolong_hbm,
        dst_ref=praw.at[2 * other],
        send_sem=near_send.at[1],
        recv_sem=near_recv.at[1],
        device_id=(beyond, other),
        device_id_type=MESH,
    )
    to_beyond.start()
    to_partner.start()
    for c in y_ring:
        pl.semaphore_signal(y_sem, inc=1, device_id=(c, core), device_id_type=MESH)

    fill_masks(slot_mask, side_mask)
    small[0].wait()
    fill_onehot(dims, (z, x, y), owner_ref, onehot)
    own.wait()
    relay_p(1, True, praw, stage, nat, window, qperm)
    small[1].wait()
    fill_turned(chip, agg_ref, qperm, turned)

    for i in range(KT):
        fetches[i].wait()

        def relay(g, carry):
            relay_a(g, a_ref, stage, left)
            return carry

        lax.fori_loop(2 * i, 2 * i + 2, relay, 0)

    pl.semaphore_wait(y_sem, ny - 1)
    for c in x_ring:
        pl.semaphore_signal(x_sem, inc=1, device_id=(c, core), device_id_type=MESH)

    to_partner.wait_recv()
    relay_p(2 * other, False, praw, stage, nat, window, qperm)
    to_beyond.wait_recv()
    relay_p(2 * core, False, praw, stage, nat, window, qperm)

    small[2].wait()
    small[3].wait()
    base = (chip * 2 + core - 1) * FB

    def rows_step(g, carry):
        fine_rows(g, base, cols_ref, slots_ref, left, window, slot_mask, side_mask, summed)
        return carry

    lax.fori_loop(0, FB // TOGETHER, rows_step, 0)
    exchanges = []
    for i, h in enumerate((other, core)):
        for j in range(PIECES):
            rows = pl.ds(j * (ROWS // PIECES), ROWS // PIECES)
            part[i, rows, :] = jnp.dot(
                turned[rows, :],
                summed[:, pl.ds(pl.multiple_of(h * HALF, HALF), HALF)],
                preferred_element_type=F32,
            )
            if i == 0:
                exchange = pltpu.make_async_remote_copy(
                    src_ref=part.at[0, rows],
                    dst_ref=theirs.at[rows],
                    send_sem=pair_send.at[j],
                    recv_sem=pair_recv.at[j],
                    device_id=(chip, other),
                    device_id_type=MESH,
                )
                exchange.start()
                exchanges.append(exchange)

    planes = plane_order(dims, z)

    def column(i, carry):
        there = column_order(i, dims, x, y)
        for u in range(nz):

            def send(u=u):
                pltpu.make_async_remote_copy(
                    src_ref=outbox.at[i * nz + u],
                    dst_ref=out_ref.at[chip, core],
                    send_sem=out_send,
                    recv_sem=out_recv.at[z],
                    device_id=(planes[u] + there, core),
                    device_id_type=MESH,
                ).start()

            if u < nz - 1:
                send()
            else:
                pl.when(i < plane - 1)(send)
        return carry

    pl.semaphore_wait(x_sem, nx - 1)
    for exchange in exchanges:
        exchange.wait_recv()
    whole = (part[1] + theirs[...]).astype(BF16)
    n = min(SENDS, chips)
    for i in range(chips // n):
        place(i, n, whole, onehot, outbox)
        lax.fori_loop(i * n // nz, (i + 1) * n // nz, column, 0)
    last = chips - 1
    pltpu.make_async_copy(outbox.at[last], out_ref.at[chip, core], out_recv.at[z]).start()

    forwards = []
    for i in range(nz):
        there = (z + i) % nz
        arrived = out_ref.at[pl.ds(there * plane, plane), core]
        pltpu.make_async_copy(arrived, arrived, out_recv.at[there]).wait()
        forward = pltpu.make_async_remote_copy(
            src_ref=arrived,
            dst_ref=arrived,
            send_sem=fwd_send.at[there],
            recv_sem=fwd_recv.at[there],
            device_id=(chip, other),
            device_id_type=MESH,
        )
        forward.start()
        forwards.append(forward)
    sent = outbox.at[pl.ds(0, chips - 1)]
    pltpu.make_async_copy(sent, sent, out_send).wait()
    to_partner.wait_send()
    to_beyond.wait_send()
    for exchange in exchanges:
        exchange.wait_send()
    for i in range(nz):
        forwards[i].wait_send()
        theirs_there = out_ref.at[pl.ds((z + i) % nz * plane, plane), other]
        pltpu.make_async_copy(theirs_there, theirs_there, fwd_recv.at[(z + i) % nz]).wait()


def shards(dims, a_blocks, a_cols, slots, prolong, aggregate, owner):
    chips = dims[0] * dims[1] * dims[2]
    hbm = pl.BlockSpec(memory_space=pltpu.HBM)
    vmem = pl.BlockSpec(memory_space=pltpu.VMEM)
    dma = pltpu.SemaphoreType.DMA
    arrived = pl.pallas_call(
        functools.partial(kernel, dims),
        out_shape=jax.ShapeDtypeStruct((chips, 2, 8, 128), BF16),
        in_specs=[hbm] * 6,
        out_specs=vmem,
        scratch_shapes=[
            pltpu.SMEM((FB, KA), jnp.int32),
            pltpu.SMEM((FB, KA), jnp.int32),
            pltpu.SMEM((FB,), jnp.int32),
            pltpu.VMEM((1, ROWS), jnp.int32),
            pltpu.VMEM((KA, FB, BS * BS), BF16),
            pltpu.VMEM((3, FB, BS * BS), BF16),
            pltpu.VMEM((2, 32 * 32, 128), F32),
            pltpu.VMEM((4, BS, 128), F32),
            pltpu.VMEM((FB, BS, KT * 256), BF16),
            pltpu.VMEM((3 * FB, BS, 128), BF16),
            pltpu.VMEM((KC, 16, HALF), BF16),
            pltpu.VMEM((KC * KC, 16, HALF), BF16),
            pltpu.VMEM((FB * BS, 128), F32),
            pltpu.VMEM((ROWS, FB * BS), BF16),
            pltpu.VMEM((FB * BS, COLS), BF16),
            pltpu.VMEM((chips * 8, ROWS), BF16),
            pltpu.VMEM((2, ROWS, HALF), F32),
            pltpu.VMEM((ROWS, HALF), F32),
            pltpu.VMEM((chips, 8, 128), BF16),
            dma((KT,)),
            dma,
            dma((4,)),
            dma((2,)),
            dma((2,)),
            dma((PIECES,)),
            dma((PIECES,)),
            dma,
            dma((dims[0],)),
            dma((dims[0],)),
            dma((dims[0],)),
            pltpu.SemaphoreType.REGULAR,
            pltpu.SemaphoreType.REGULAR,
        ],
        compiler_params=pltpu.CompilerParams(
            collective_id=0, has_side_effects=True, vmem_limit_bytes=48 * 1024 * 1024
        ),
    )(
        *[
            pltpu.with_memory_space_constraint(x, pltpu.HBM)
            for x in (
                jnp.transpose(a_blocks, (1, 0, 2)),
                a_cols,
                slots,
                prolong,
                aggregate,
                owner.reshape(1, ROWS),
            )
        ]
    )
    rows = arrived.reshape(chips, 4, MOST, 128).astype(F32)
    return jnp.transpose(rows, (0, 2, 1, 3)).reshape(1, chips, MOST, COLS)


def solution(mesh):
    in_specs = (
        P(("rows", "pair"), None, None),
        P(("rows", "pair"), None),
        P(("rows", "pair"), None),
        P(("rows", "pair"), None),
        P(("rows", "pair")),
        P("rows", None),
    )
    out_specs = P("rows", None, None, None)
    return jax.shard_map(
        functools.partial(shards, DIMS),
        mesh=mesh,
        in_specs=in_specs,
        out_specs=out_specs,
        check_vma=False,
    )
```

```python
import functools

import jax
import jax.numpy as jnp
from jax import lax
from jax.experimental import pallas as pl
from jax.experimental.pallas import tpu as pltpu
from jax.sharding import PartitionSpec as P

BS = 64
KA = 27
KC = 8
FB = 24
CB = 4
MOST = 4
ROWS = CB * BS
COLS = KC * BS
HALF = COLS // 2
KT = 7
SKEW = 25
PIECES = 2
SENDS = 32
TOGETHER = 6
DIMS = (8, 4, 4)
MESH = pl.DeviceIdType.MESH
BF16 = jnp.bfloat16
F32 = jnp.float32


def fold_blocks(one, two, low):
    top = jnp.where(low, one, pltpu.roll(two, BS, 1))
    bottom = jnp.where(low, pltpu.roll(one, BS, 1), two)
    return top, bottom


def low_lanes():
    return lax.broadcasted_iota(jnp.int32, (32, 128), 1) < BS


def relay_a(g, a_ref, stage, left):
    low = low_lanes()
    for half in range(2):
        for t in range(32):
            stage[half, pl.ds(t * SKEW, FB), :] = a_ref[
                jnp.minimum(2 * g + half, KA - 1), :, pl.ds(t * 128, 128)
            ].astype(F32)
    column = pl.ds(pl.multiple_of(g * 128, 128), 128)
    for f in range(FB):
        one = stage[0, pl.ds(f, 32, stride=SKEW), :]
        two = stage[1, pl.ds(f, 32, stride=SKEW), :]
        top, bottom = fold_blocks(one, two, low)
        left[f, pl.ds(0, 32), column] = top.astype(BF16)
        left[f, pl.ds(32, 32), column] = bottom.astype(BF16)


def relay_p(w, keep, praw, stage, nat, window, qperm):
    low = low_lanes()
    for t in range(32):
        stage[0, pl.ds(t * SKEW, FB), :] = praw[w, :, pl.ds(t * 128, 128)].astype(F32)
    for b in range(FB):
        one = stage[0, pl.ds(b, 32, stride=SKEW), :]
        top, bottom = fold_blocks(one, one, low)
        if keep:
            qperm[pl.ds(b * BS, 32), :] = top
            qperm[pl.ds(b * BS + 32, 32), :] = bottom
        nat[b % 4, pl.ds(0, 32, stride=2), :] = top
        nat[b % 4, pl.ds(1, 32, stride=2), :] = bottom
        window[w * FB + b] = nat[b % 4].astype(BF16)


def fill_masks(slot_mask, side_mask):
    column_slot = lax.broadcasted_iota(jnp.int32, (16, HALF), 1) // BS
    first = lax.broadcasted_iota(jnp.int32, (16, 128), 1) < BS
    for s in range(KC):
        slot_mask[s] = jnp.where(column_slot == s % 4, 1.0, 0.0).astype(BF16)
        for t in range(KC):
            below = jnp.where(first, 1.0 - s // 4, 1.0 - t // 4)
            side_mask[KC * s + t, :, 0:128] = below.astype(BF16)
            side_mask[KC * s + t, :, 128:256] = (1.0 - below).astype(BF16)


def spread(i, n):
    return n // 2 + (i + 1) // 2 * (1 - 2 * (i % 2))


def plane_order(dims, z, own):
    nz, nx, ny = dims
    half = nz // 2
    side = (z // half + 1 - own) % 2
    return [(side * half + (z + own + i) % half) * (nx * ny) for i in range(half)]


def column_order(i, dims, x, y):
    nz, nx, ny = dims
    return (x + spread(i // ny, nx)) % nx * ny + (y + spread(i % ny, ny)) % ny


def fill_onehot(dims, place_of, owner_ref, onehot):
    nz, nx, ny = dims
    z, x, y = place_of
    owner_row = jnp.broadcast_to(owner_ref[...].astype(F32), (128, ROWS))
    owners = jnp.transpose(owner_row)
    target = jnp.where(
        owners == lax.broadcasted_iota(jnp.int32, (ROWS, 128), 1).astype(F32), 1.0, 0.0
    )
    earlier = jnp.where(
        lax.broadcasted_iota(jnp.int32, (ROWS, ROWS), 0)
        > lax.broadcasted_iota(jnp.int32, (ROWS, ROWS), 1),
        1.0,
        0.0,
    ).astype(BF16)
    before = jnp.dot(earlier, target.astype(BF16), preferred_element_type=F32)
    rank = jnp.sum(before * target, axis=1, keepdims=True)
    key_row = jnp.transpose(owners * MOST + rank)[0:1, :]
    slot = lax.broadcasted_iota(jnp.int32, (16, ROWS), 0) % MOST
    upper = lax.broadcasted_iota(jnp.int32, (16, ROWS), 0) // 8
    half = nz // 2

    def column(own, planes, i, carry):
        there = column_order(i, dims, x, y)
        for u in range(0, half, 2):
            code = slot + (planes[u] + there) * MOST + upper * ((planes[u + 1] - planes[u]) * MOST)
            rows = pl.ds(pl.multiple_of(((own * nx * ny + i) * half + u) * 8, 16), 16)
            onehot[rows, :] = jnp.where(code.astype(F32) == key_row, 1.0, 0.0).astype(BF16)
        return carry

    for own in range(2):
        planes = plane_order(dims, z, own)
        lax.fori_loop(0, nx * ny, functools.partial(column, own, planes), 0)


def fill_turned(chip, agg_ref, qperm, turned):
    wide = lax.broadcasted_iota(jnp.int32, (128, 128), 1) < BS
    tall = lax.broadcasted_iota(jnp.int32, (128, 128), 0) // BS
    for g in range(FB // 2):
        block = jnp.transpose(qperm[pl.ds(g * 128, 128), :])
        member = jnp.where(wide, agg_ref[2 * g], agg_ref[2 * g + 1]) - chip * CB
        for u in range(CB // 2):
            turned[pl.ds(u * 128, 128), pl.ds(g * 128, 128)] = jnp.where(
                member == tall + 2 * u, block, 0.0
            ).astype(BF16)


def tall(mask):
    return jnp.concatenate([mask] * (BS // 16), axis=0)


def positions(f, kk, base, cols_ref, slots_ref, left, window, slot_mask, side_mask):
    blocks, low, high = [], [], []
    for k in (4 * kk, 4 * kk + 2):
        slots = [slots_ref[f, min(k + i, KA - 1)] for i in range(2)]
        for i in range(2):
            if k + i < KA:
                block = window[jnp.clip(cols_ref[f, k + i] - base, 0, 3 * FB - 1)]
                keep = tall(slot_mask[slots[i]])
                blocks.append(jnp.concatenate([block, block], axis=1) * keep)
            else:
                blocks.append(jnp.zeros((BS, HALF), BF16))
        pair = left[f, :, pl.ds(k * BS, 128)]
        keep = side_mask[slots[0] * KC + slots[1]]
        low.append(pair * tall(keep[:, 0:128]))
        high.append(pair * tall(keep[:, 128:256]))
    rows = [jnp.concatenate(low, axis=1), jnp.concatenate(high, axis=1)]
    return jnp.dot(
        jnp.concatenate(rows, axis=0),
        jnp.concatenate(blocks, axis=0),
        preferred_element_type=F32,
    )


def fine_rows(g, base, cols_ref, slots_ref, left, window, slot_mask, side_mask, summed):
    total = [None] * TOGETHER
    for kk in range(KT):
        for i in range(TOGETHER):
            f = g * TOGETHER + i
            term = positions(
                f, kk, base, cols_ref, slots_ref, left, window, slot_mask, side_mask
            )
            total[i] = term if kk == 0 else total[i] + term
    for i in range(TOGETHER):
        rows = pl.ds(pl.multiple_of((g * TOGETHER + i) * BS, BS), BS)
        summed[rows, 0:HALF] = total[i][0:BS].astype(BF16)
        summed[rows, HALF:COLS] = total[i][BS:].astype(BF16)


def place(i, n, whole, onehot, outbox):
    first = (lax.broadcasted_iota(jnp.int32, (8 * n, 128), 0) // MOST) % 2 == 0
    placed = jnp.dot(onehot[pl.ds(i * 8 * n, 8 * n), :], whole, preferred_element_type=F32)
    value = jnp.where(first, placed[:, 0:128], placed[:, 128:256])
    for j in range(n):
        outbox[i * n + j] = value[j * 8 : (j + 1) * 8].astype(BF16)


def kernel(
    dims,
    a_hbm,
    cols_hbm,
    slots_hbm,
    prolong_hbm,
    agg_hbm,
    owner_hbm,
    out_ref,
    cols_ref,
    slots_ref,
    agg_ref,
    owner_ref,
    a_ref,
    praw,
    stage,
    nat,
    left,
    window,
    slot_mask,
    side_mask,
    qperm,
    turned,
    summed,
    onehot,
    part,
    theirs,
    outbox,
    a_sem,
    p_sem,
    small_sem,
    near_send,
    near_recv,
    pair_send,
    pair_recv,
    out_send,
    out_recv,
    fwd_send,
    fwd_recv,
    ring_sem,
):
    nz, nx, ny = dims
    chips = nz * nx * ny
    plane = nx * ny
    chip = lax.axis_index("rows")
    core = lax.axis_index("pair")
    other = 1 - core
    z, x, y = chip // (nx * ny), (chip // ny) % nx, chip % ny
    beyond = chip - 1 + 2 * core
    has_beyond = jnp.logical_and(beyond >= 0, beyond < chips)

    z_ring = [((z + i) % nz * nx + x) * ny + y for i in range(1, nz)]
    x_ring = [(z * nx + (x + i) % nx) * ny + y for i in range(1, nx)]
    y_ring = [(z * nx + x) * ny + (y + i) % ny for i in range(1, ny)]

    def signal_ring(sem, ring):
        for there in ring:
            pl.semaphore_signal(sem, inc=1, device_id=(there, core), device_id_type=MESH)

    barrier = pltpu.get_barrier_semaphore()
    pl.semaphore_signal(barrier, inc=1, device_id=(chip, other), device_id_type=MESH)

    @pl.when(has_beyond)
    def _():
        pl.semaphore_signal(barrier, inc=1, device_id=(beyond, other), device_id_type=MESH)

    signal_ring(barrier, y_ring + x_ring + z_ring)
    fetches = []
    for i in range(KT):
        span = pl.ds(4 * i, min(4, KA - 4 * i))
        fetches.append(pltpu.make_async_copy(a_hbm.at[span], a_ref.at[span], a_sem.at[i]))
    own = pltpu.make_async_copy(prolong_hbm, praw.at[1], p_sem)
    own.start()
    small = [
        pltpu.make_async_copy(src, dst, small_sem.at[i])
        for i, (src, dst) in enumerate(
            [
                (owner_hbm, owner_ref),
                (agg_hbm, agg_ref),
                (cols_hbm, cols_ref),
                (slots_hbm, slots_ref),
            ]
        )
    ]
    for copy in small:
        copy.start()

    fill_masks(slot_mask, side_mask)
    pl.semaphore_wait(
        barrier,
        1 + has_beyond.astype(jnp.int32) + nz + nx + ny - 3,
    )

    own.wait()
    to_partner = pltpu.make_async_remote_copy(
        src_ref=praw.at[1],
        dst_ref=praw.at[2 * core],
        send_sem=near_send.at[0],
        recv_sem=near_recv.at[0],
        device_id=(chip, other),
        device_id_type=MESH,
    )
    to_beyond = pltpu.make_async_remote_copy(
        src_ref=praw.at[1],
        dst_ref=praw.at[2 * other],
        send_sem=near_send.at[1],
        recv_sem=near_recv.at[1],
        device_id=(beyond, other),
        device_id_type=MESH,
    )
    pl.when(has_beyond)(to_beyond.start)
    to_partner.start()
    for fetch in fetches:
        fetch.start()
    signal_ring(ring_sem.at[0], y_ring)

    relay_p(1, True, praw, stage, nat, window, qperm)
    small[1].wait()
    fill_turned(chip, agg_ref, qperm, turned)

    for i in range(KT):
        fetches[i].wait()

        def relay(g, carry):
            relay_a(g, a_ref, stage, left)
            return carry

        lax.fori_loop(2 * i, 2 * i + 2, relay, 0)

    pl.semaphore_wait(ring_sem.at[0], ny - 1)
    signal_ring(ring_sem.at[1], x_ring)
    to_partner.wait_recv()
    relay_p(2 * other, False, praw, stage, nat, window, qperm)
    pl.when(has_beyond)(to_beyond.wait_recv)
    relay_p(2 * core, False, praw, stage, nat, window, qperm)

    small[2].wait()
    small[3].wait()
    base = (chip * 2 + core - 1) * FB

    def rows_step(g, carry):
        fine_rows(g, base, cols_ref, slots_ref, left, window, slot_mask, side_mask, summed)
        return carry

    lax.fori_loop(0, FB // TOGETHER, rows_step, 0)
    exchanges = []
    for i, h in enumerate((other, core)):
        for j in range(PIECES):
            rows = pl.ds(j * (ROWS // PIECES), ROWS // PIECES)
            part[i, rows, :] = jnp.dot(
                turned[rows, :],
                summed[:, pl.ds(pl.multiple_of(h * HALF, HALF), HALF)],
                preferred_element_type=F32,
            )
            if i == 0:
                exchange = pltpu.make_async_remote_copy(
                    src_ref=part.at[0, rows],
                    dst_ref=theirs.at[rows],
                    send_sem=pair_send.at[j],
                    recv_sem=pair_recv.at[j],
                    device_id=(chip, other),
                    device_id_type=MESH,
                )
                exchange.start()
                exchanges.append(exchange)

    span = nz // 2

    def column(own, planes, i, carry):
        there = column_order(i, dims, x, y)
        for u in range(span):

            def send(u=u):
                pltpu.make_async_remote_copy(
                    src_ref=outbox.at[(own * plane + i) * span + u],
                    dst_ref=out_ref.at[chip, core],
                    send_sem=out_send,
                    recv_sem=out_recv.at[z],
                    device_id=(planes[u] + there, core),
                    device_id_type=MESH,
                ).start()

            if own == 0 or u < span - 1:
                send()
            else:
                pl.when(i < plane - 1)(send)
        return carry

    small[0].wait()
    fill_onehot(dims, (z, x, y), owner_ref, onehot)
    pl.semaphore_wait(ring_sem.at[1], nx - 1)
    for exchange in exchanges:
        exchange.wait_recv()
    whole = (part[1] + theirs[...]).astype(BF16)
    n = min(SENDS, chips)
    for i in range(chips // n):
        place(i, n, whole, onehot, outbox)
        own, first = divmod(i * n // span, plane)
        step = functools.partial(column, own, plane_order(dims, z, own))
        lax.fori_loop(first, first + n // span, step, 0)
    last = chips - 1
    pltpu.make_async_copy(outbox.at[last], out_ref.at[chip, core], out_recv.at[z]).start()

    forwards = []
    for i in range(nz):
        there = (z + i) % nz
        arrived = out_ref.at[pl.ds(there * plane, plane), core]
        pltpu.make_async_copy(arrived, arrived, out_recv.at[there]).wait()
        forward = pltpu.make_async_remote_copy(
            src_ref=arrived,
            dst_ref=arrived,
            send_sem=fwd_send.at[there],
            recv_sem=fwd_recv.at[there],
            device_id=(chip, other),
            device_id_type=MESH,
        )
        forward.start()
        forwards.append(forward)
    sent = outbox.at[pl.ds(0, chips - 1)]
    pltpu.make_async_copy(sent, sent, out_send).wait()
    to_partner.wait_send()
    pl.when(has_beyond)(to_beyond.wait_send)
    for exchange in exchanges:
        exchange.wait_send()
    for i in range(nz):
        forwards[i].wait_send()
        theirs_there = out_ref.at[pl.ds((z + i) % nz * plane, plane), other]
        pltpu.make_async_copy(theirs_there, theirs_there, fwd_recv.at[(z + i) % nz]).wait()


def shards(dims, a_blocks, a_cols, slots, prolong, aggregate, owner):
    chips = dims[0] * dims[1] * dims[2]
    hbm = pl.BlockSpec(memory_space=pltpu.HBM)
    vmem = pl.BlockSpec(memory_space=pltpu.VMEM)
    dma = pltpu.SemaphoreType.DMA
    arrived = pl.pallas_call(
        functools.partial(kernel, dims),
        out_shape=jax.ShapeDtypeStruct((chips, 2, 8, 128), BF16),
        in_specs=[hbm] * 6,
        out_specs=vmem,
        scratch_shapes=[
            pltpu.SMEM((FB, KA), jnp.int32),
            pltpu.SMEM((FB, KA), jnp.int32),
            pltpu.SMEM((FB,), jnp.int32),
            pltpu.VMEM((1, ROWS), jnp.int32),
            pltpu.VMEM((KA, FB, BS * BS), BF16),
            pltpu.VMEM((3, FB, BS * BS), BF16),
            pltpu.VMEM((2, 32 * 32, 128), F32),
            pltpu.VMEM((4, BS, 128), F32),
            pltpu.VMEM((FB, BS, KT * 256), BF16),
            pltpu.VMEM((3 * FB, BS, 128), BF16),
            pltpu.VMEM((KC, 16, HALF), BF16),
            pltpu.VMEM((KC * KC, 16, HALF), BF16),
            pltpu.VMEM((FB * BS, 128), F32),
            pltpu.VMEM((ROWS, FB * BS), BF16),
            pltpu.VMEM((FB * BS, COLS), BF16),
            pltpu.VMEM((chips * 8, ROWS), BF16),
            pltpu.VMEM((2, ROWS, HALF), F32),
            pltpu.VMEM((ROWS, HALF), F32),
            pltpu.VMEM((chips, 8, 128), BF16),
            dma((KT,)),
            dma,
            dma((4,)),
            dma((2,)),
            dma((2,)),
            dma((PIECES,)),
            dma((PIECES,)),
            dma,
            dma((dims[0],)),
            dma((dims[0],)),
            dma((dims[0],)),
            pltpu.SemaphoreType.REGULAR((2,)),
        ],
        compiler_params=pltpu.CompilerParams(
            collective_id=0, has_side_effects=True, vmem_limit_bytes=48 * 1024 * 1024
        ),
    )(
        *[
            pltpu.with_memory_space_constraint(x, pltpu.HBM)
            for x in (
                jnp.transpose(a_blocks, (1, 0, 2)),
                a_cols,
                slots,
                prolong,
                aggregate,
                owner.reshape(1, ROWS),
            )
        ]
    )
    rows = arrived.reshape(chips, 4, MOST, 128).astype(F32)
    return jnp.transpose(rows, (0, 2, 1, 3)).reshape(1, chips, MOST, COLS)


def solution(mesh):
    in_specs = (
        P(("rows", "pair"), None, None),
        P(("rows", "pair"), None),
        P(("rows", "pair"), None),
        P(("rows", "pair"), None),
        P(("rows", "pair")),
        P("rows", None),
    )
    out_specs = P("rows", None, None, None)
    return jax.shard_map(
        functools.partial(shards, DIMS),
        mesh=mesh,
        in_specs=in_specs,
        out_specs=out_specs,
        check_vma=False,
    )
```

```python
import functools

import jax
import jax.numpy as jnp
from jax import lax
from jax.experimental import pallas as pl
from jax.experimental.pallas import tpu as pltpu
from jax.sharding import PartitionSpec as P

BS = 64
KA = 27
KC = 8
FB = 24
CB = 4
MOST = 4
ROWS = CB * BS
COLS = KC * BS
HALF = COLS // 2
KT = 7
SKEW = 25
PIECES = 1
SENDS = 32
TOGETHER = 12
DIMS = (8, 4, 4)
MESH = pl.DeviceIdType.MESH
BF16 = jnp.bfloat16
F32 = jnp.float32


def fold_blocks(one, two, low):
    top = jnp.where(low, one, pltpu.roll(two, BS, 1))
    bottom = jnp.where(low, pltpu.roll(one, BS, 1), two)
    return top, bottom


def low_lanes():
    return lax.broadcasted_iota(jnp.int32, (32, 128), 1) < BS


def relay_a(g, a_ref, stage, left):
    low = low_lanes()
    for half in range(2):
        for t in range(32):
            stage[half, pl.ds(t * SKEW, FB), :] = a_ref[
                jnp.minimum(2 * g + half, KA - 1), :, pl.ds(t * 128, 128)
            ].astype(F32)
    column = pl.ds(pl.multiple_of(g * 128, 128), 128)
    for f in range(FB):
        one = stage[0, pl.ds(f, 32, stride=SKEW), :]
        two = stage[1, pl.ds(f, 32, stride=SKEW), :]
        top, bottom = fold_blocks(one, two, low)
        left[f, pl.ds(0, 32), column] = top.astype(BF16)
        left[f, pl.ds(32, 32), column] = bottom.astype(BF16)


def relay_p(w, keep, praw, stage, nat, window, qperm):
    low = low_lanes()
    for t in range(32):
        stage[0, pl.ds(t * SKEW, FB), :] = praw[w, :, pl.ds(t * 128, 128)].astype(F32)
    for b in range(FB):
        one = stage[0, pl.ds(b, 32, stride=SKEW), :]
        top, bottom = fold_blocks(one, one, low)
        if keep:
            qperm[pl.ds(b * BS, 32), :] = top
            qperm[pl.ds(b * BS + 32, 32), :] = bottom
        nat[b % 4, pl.ds(0, 32, stride=2), :] = top
        nat[b % 4, pl.ds(1, 32, stride=2), :] = bottom
        window[w * FB + b] = nat[b % 4].astype(BF16)


def fill_masks(slot_mask, side_mask):
    column_slot = lax.broadcasted_iota(jnp.int32, (16, HALF), 1) // BS
    first = lax.broadcasted_iota(jnp.int32, (16, 128), 1) < BS
    for s in range(KC):
        slot_mask[s] = jnp.where(column_slot == s % 4, 1.0, 0.0).astype(BF16)
        for t in range(KC):
            below = jnp.where(first, 1.0 - s // 4, 1.0 - t // 4)
            side_mask[KC * s + t, :, 0:128] = below.astype(BF16)
            side_mask[KC * s + t, :, 128:256] = (1.0 - below).astype(BF16)


def spread(i, n):
    return n // 2 + (i + 1) // 2 * (1 - 2 * (i % 2))


def plane_order(dims, z, own):
    nz, nx, ny = dims
    half = nz // 2
    side = (z // half + 1 - own) % 2
    return [(side * half + (z + own + i) % half) * (nx * ny) for i in range(half)]


def column_order(i, dims, x, y):
    nz, nx, ny = dims
    return (x + spread(i // ny, nx)) % nx * ny + (y + spread(i % ny, ny)) % ny


def fill_onehot(dims, place_of, owner_ref, onehot):
    nz, nx, ny = dims
    z, x, y = place_of
    owner_row = jnp.broadcast_to(owner_ref[...].astype(F32), (128, ROWS))
    owners = jnp.transpose(owner_row)
    target = jnp.where(
        owners == lax.broadcasted_iota(jnp.int32, (ROWS, 128), 1).astype(F32), 1.0, 0.0
    )
    earlier = jnp.where(
        lax.broadcasted_iota(jnp.int32, (ROWS, ROWS), 0)
        > lax.broadcasted_iota(jnp.int32, (ROWS, ROWS), 1),
        1.0,
        0.0,
    ).astype(BF16)
    before = jnp.dot(earlier, target.astype(BF16), preferred_element_type=F32)
    rank = jnp.sum(before * target, axis=1, keepdims=True)
    key_row = jnp.transpose(owners * MOST + rank)[0:1, :]
    slot = lax.broadcasted_iota(jnp.int32, (16, ROWS), 0) % MOST
    upper = lax.broadcasted_iota(jnp.int32, (16, ROWS), 0) // 8
    half = nz // 2

    def column(own, planes, i, carry):
        there = column_order(i, dims, x, y)
        for u in range(0, half, 2):
            code = slot + (planes[u] + there) * MOST + upper * ((planes[u + 1] - planes[u]) * MOST)
            rows = pl.ds(pl.multiple_of(((own * nx * ny + i) * half + u) * 8, 16), 16)
            onehot[rows, :] = jnp.where(code.astype(F32) == key_row, 1.0, 0.0).astype(BF16)
        return carry

    for own in range(2):
        planes = plane_order(dims, z, own)
        lax.fori_loop(0, nx * ny, functools.partial(column, own, planes), 0)


def fill_turned(chip, agg_ref, qperm, turned):
    wide = lax.broadcasted_iota(jnp.int32, (128, 128), 1) < BS
    tall = lax.broadcasted_iota(jnp.int32, (128, 128), 0) // BS
    for g in range(FB // 2):
        block = jnp.transpose(qperm[pl.ds(g * 128, 128), :])
        member = jnp.where(wide, agg_ref[2 * g], agg_ref[2 * g + 1]) - chip * CB
        for u in range(CB // 2):
            turned[pl.ds(u * 128, 128), pl.ds(g * 128, 128)] = jnp.where(
                member == tall + 2 * u, block, 0.0
            ).astype(BF16)


def tall(mask):
    return jnp.concatenate([mask] * (BS // 16), axis=0)


def positions(f, kk, base, cols_ref, slots_ref, left, window, slot_mask, side_mask):
    blocks, low, high = [], [], []
    for k in (4 * kk, 4 * kk + 2):
        slots = [slots_ref[f, min(k + i, KA - 1)] for i in range(2)]
        for i in range(2):
            if k + i < KA:
                block = window[jnp.clip(cols_ref[f, k + i] - base, 0, 3 * FB - 1)]
                keep = tall(slot_mask[slots[i]])
                blocks.append(jnp.concatenate([block, block], axis=1) * keep)
            else:
                blocks.append(jnp.zeros((BS, HALF), BF16))
        pair = left[f, :, pl.ds(k * BS, 128)]
        keep = side_mask[slots[0] * KC + slots[1]]
        low.append(pair * tall(keep[:, 0:128]))
        high.append(pair * tall(keep[:, 128:256]))
    rows = [jnp.concatenate(low, axis=1), jnp.concatenate(high, axis=1)]
    return jnp.dot(
        jnp.concatenate(rows, axis=0),
        jnp.concatenate(blocks, axis=0),
        preferred_element_type=F32,
    )


def fine_rows(g, base, cols_ref, slots_ref, left, window, slot_mask, side_mask, summed):
    total = [None] * TOGETHER
    for kk in range(KT):
        for i in range(TOGETHER):
            f = g * TOGETHER + i
            term = positions(
                f, kk, base, cols_ref, slots_ref, left, window, slot_mask, side_mask
            )
            total[i] = term if kk == 0 else total[i] + term
    for i in range(TOGETHER):
        rows = pl.ds(pl.multiple_of((g * TOGETHER + i) * BS, BS), BS)
        summed[rows, 0:HALF] = total[i][0:BS].astype(BF16)
        summed[rows, HALF:COLS] = total[i][BS:].astype(BF16)


def place(i, n, whole, onehot, outbox):
    first = (lax.broadcasted_iota(jnp.int32, (8 * n, 128), 0) // MOST) % 2 == 0
    placed = jnp.dot(onehot[pl.ds(i * 8 * n, 8 * n), :], whole, preferred_element_type=F32)
    value = jnp.where(first, placed[:, 0:128], placed[:, 128:256])
    for j in range(n):
        outbox[i * n + j] = value[j * 8 : (j + 1) * 8].astype(BF16)


def kernel(
    dims,
    a_hbm,
    cols_hbm,
    slots_hbm,
    prolong_hbm,
    agg_hbm,
    owner_hbm,
    out_ref,
    cols_ref,
    slots_ref,
    agg_ref,
    owner_ref,
    a_ref,
    praw,
    stage,
    nat,
    left,
    window,
    slot_mask,
    side_mask,
    qperm,
    turned,
    summed,
    onehot,
    part,
    theirs,
    outbox,
    a_sem,
    p_sem,
    small_sem,
    near_send,
    near_recv,
    pair_send,
    pair_recv,
    out_send,
    out_recv,
    fwd_send,
    fwd_recv,
    ring_sem,
):
    nz, nx, ny = dims
    chips = nz * nx * ny
    plane = nx * ny
    chip = lax.axis_index("rows")
    core = lax.axis_index("pair")
    other = 1 - core
    z, x, y = chip // (nx * ny), (chip // ny) % nx, chip % ny
    beyond = chip - 1 + 2 * core
    has_beyond = jnp.logical_and(beyond >= 0, beyond < chips)

    z_ring = [((z + i) % nz * nx + x) * ny + y for i in range(1, nz)]
    x_ring = [(z * nx + (x + i) % nx) * ny + y for i in range(1, nx)]
    y_ring = [(z * nx + x) * ny + (y + i) % ny for i in range(1, ny)]

    def signal_ring(sem, ring):
        for there in ring:
            pl.semaphore_signal(sem, inc=1, device_id=(there, core), device_id_type=MESH)

    barrier = pltpu.get_barrier_semaphore()
    pl.semaphore_signal(barrier, inc=1, device_id=(chip, other), device_id_type=MESH)

    @pl.when(has_beyond)
    def _():
        pl.semaphore_signal(barrier, inc=1, device_id=(beyond, other), device_id_type=MESH)

    signal_ring(barrier, y_ring + x_ring + z_ring)
    fetches = []
    for i in range(KT):
        span = pl.ds(4 * i, min(4, KA - 4 * i))
        fetches.append(pltpu.make_async_copy(a_hbm.at[span], a_ref.at[span], a_sem.at[i]))
    own = pltpu.make_async_copy(prolong_hbm, praw.at[1], p_sem)
    own.start()
    small = [
        pltpu.make_async_copy(src, dst, small_sem.at[i])
        for i, (src, dst) in enumerate(
            [
                (owner_hbm, owner_ref),
                (agg_hbm, agg_ref),
                (cols_hbm, cols_ref),
                (slots_hbm, slots_ref),
            ]
        )
    ]
    for copy in small:
        copy.start()

    fill_masks(slot_mask, side_mask)
    pl.semaphore_wait(
        barrier,
        1 + has_beyond.astype(jnp.int32) + nz + nx + ny - 3,
    )

    own.wait()
    to_partner = pltpu.make_async_remote_copy(
        src_ref=praw.at[1],
        dst_ref=praw.at[2 * core],
        send_sem=near_send.at[0],
        recv_sem=near_recv.at[0],
        device_id=(chip, other),
        device_id_type=MESH,
    )
    to_beyond = pltpu.make_async_remote_copy(
        src_ref=praw.at[1],
        dst_ref=praw.at[2 * other],
        send_sem=near_send.at[1],
        recv_sem=near_recv.at[1],
        device_id=(beyond, other),
        device_id_type=MESH,
    )
    pl.when(has_beyond)(to_beyond.start)
    to_partner.start()
    for fetch in fetches:
        fetch.start()
    signal_ring(ring_sem.at[0], y_ring)

    relay_p(1, True, praw, stage, nat, window, qperm)
    small[1].wait()
    fill_turned(chip, agg_ref, qperm, turned)

    for i in range(KT):
        fetches[i].wait()

        def relay(g, carry):
            relay_a(g, a_ref, stage, left)
            return carry

        lax.fori_loop(2 * i, 2 * i + 2, relay, 0)

    pl.semaphore_wait(ring_sem.at[0], ny - 1)
    signal_ring(ring_sem.at[1], x_ring)
    to_partner.wait_recv()
    relay_p(2 * other, False, praw, stage, nat, window, qperm)
    pl.when(has_beyond)(to_beyond.wait_recv)
    relay_p(2 * core, False, praw, stage, nat, window, qperm)

    small[2].wait()
    small[3].wait()
    base = (chip * 2 + core - 1) * FB

    def rows_step(g, carry):
        fine_rows(g, base, cols_ref, slots_ref, left, window, slot_mask, side_mask, summed)
        return carry

    lax.fori_loop(0, FB // TOGETHER, rows_step, 0)
    exchanges = []
    for i, h in enumerate((other, core)):
        for j in range(PIECES):
            rows = pl.ds(j * (ROWS // PIECES), ROWS // PIECES)
            part[i, rows, :] = jnp.dot(
                turned[rows, :],
                summed[:, pl.ds(pl.multiple_of(h * HALF, HALF), HALF)],
                preferred_element_type=F32,
            )
            if i == 0:
                exchange = pltpu.make_async_remote_copy(
                    src_ref=part.at[0, rows],
                    dst_ref=theirs.at[rows],
                    send_sem=pair_send.at[j],
                    recv_sem=pair_recv.at[j],
                    device_id=(chip, other),
                    device_id_type=MESH,
                )
                exchange.start()
                exchanges.append(exchange)

    span = nz // 2

    def column(own, planes, i, carry):
        there = column_order(i, dims, x, y)
        for u in range(span):

            def send(u=u):
                pltpu.make_async_remote_copy(
                    src_ref=outbox.at[(own * plane + i) * span + u],
                    dst_ref=out_ref.at[chip, core],
                    send_sem=out_send,
                    recv_sem=out_recv.at[z],
                    device_id=(planes[u] + there, core),
                    device_id_type=MESH,
                ).start()

            if own == 0 or u < span - 1:
                send()
            else:
                pl.when(i < plane - 1)(send)
        return carry

    small[0].wait()
    fill_onehot(dims, (z, x, y), owner_ref, onehot)
    pl.semaphore_wait(ring_sem.at[1], nx - 1)
    for exchange in exchanges:
        exchange.wait_recv()
    whole = (part[1] + theirs[...]).astype(BF16)
    n = min(SENDS, chips)
    for i in range(chips // n):
        place(i, n, whole, onehot, outbox)
        own, first = divmod(i * n // span, plane)
        step = functools.partial(column, own, plane_order(dims, z, own))
        lax.fori_loop(first, first + n // span, step, 0)
    last = chips - 1
    pltpu.make_async_copy(outbox.at[last], out_ref.at[chip, core], out_recv.at[z]).start()

    forwards = []
    for i in range(nz):
        there = (z + i) % nz
        arrived = out_ref.at[pl.ds(there * plane, plane), core]
        pltpu.make_async_copy(arrived, arrived, out_recv.at[there]).wait()
        forward = pltpu.make_async_remote_copy(
            src_ref=arrived,
            dst_ref=arrived,
            send_sem=fwd_send.at[there],
            recv_sem=fwd_recv.at[there],
            device_id=(chip, other),
            device_id_type=MESH,
        )
        forward.start()
        forwards.append(forward)
    sent = outbox.at[pl.ds(0, chips - 1)]
    pltpu.make_async_copy(sent, sent, out_send).wait()
    to_partner.wait_send()
    pl.when(has_beyond)(to_beyond.wait_send)
    for exchange in exchanges:
        exchange.wait_send()
    for i in range(nz):
        forwards[i].wait_send()
        theirs_there = out_ref.at[pl.ds((z + i) % nz * plane, plane), other]
        pltpu.make_async_copy(theirs_there, theirs_there, fwd_recv.at[(z + i) % nz]).wait()


def shards(dims, a_blocks, a_cols, slots, prolong, aggregate, owner):
    chips = dims[0] * dims[1] * dims[2]
    hbm = pl.BlockSpec(memory_space=pltpu.HBM)
    vmem = pl.BlockSpec(memory_space=pltpu.VMEM)
    dma = pltpu.SemaphoreType.DMA
    arrived = pl.pallas_call(
        functools.partial(kernel, dims),
        out_shape=jax.ShapeDtypeStruct((chips, 2, 8, 128), BF16),
        in_specs=[hbm] * 6,
        out_specs=vmem,
        scratch_shapes=[
            pltpu.SMEM((FB, KA), jnp.int32),
            pltpu.SMEM((FB, KA), jnp.int32),
            pltpu.SMEM((FB,), jnp.int32),
            pltpu.VMEM((1, ROWS), jnp.int32),
            pltpu.VMEM((KA, FB, BS * BS), BF16),
            pltpu.VMEM((3, FB, BS * BS), BF16),
            pltpu.VMEM((2, 32 * 32, 128), F32),
            pltpu.VMEM((4, BS, 128), F32),
            pltpu.VMEM((FB, BS, KT * 256), BF16),
            pltpu.VMEM((3 * FB, BS, 128), BF16),
            pltpu.VMEM((KC, 16, HALF), BF16),
            pltpu.VMEM((KC * KC, 16, HALF), BF16),
            pltpu.VMEM((FB * BS, 128), F32),
            pltpu.VMEM((ROWS, FB * BS), BF16),
            pltpu.VMEM((FB * BS, COLS), BF16),
            pltpu.VMEM((chips * 8, ROWS), BF16),
            pltpu.VMEM((2, ROWS, HALF), F32),
            pltpu.VMEM((ROWS, HALF), F32),
            pltpu.VMEM((chips, 8, 128), BF16),
            dma((KT,)),
            dma,
            dma((4,)),
            dma((2,)),
            dma((2,)),
            dma((PIECES,)),
            dma((PIECES,)),
            dma,
            dma((dims[0],)),
            dma((dims[0],)),
            dma((dims[0],)),
            pltpu.SemaphoreType.REGULAR((2,)),
        ],
        compiler_params=pltpu.CompilerParams(
            collective_id=0, has_side_effects=True, vmem_limit_bytes=48 * 1024 * 1024
        ),
    )(
        *[
            pltpu.with_memory_space_constraint(x, pltpu.HBM)
            for x in (
                jnp.transpose(a_blocks, (1, 0, 2)),
                a_cols,
                slots,
                prolong,
                aggregate,
                owner.reshape(1, ROWS),
            )
        ]
    )
    rows = arrived.reshape(chips, 4, MOST, 128).astype(F32)
    return jnp.transpose(rows, (0, 2, 1, 3)).reshape(1, chips, MOST, COLS)


def solution(mesh):
    in_specs = (
        P(("rows", "pair"), None, None),
        P(("rows", "pair"), None),
        P(("rows", "pair"), None),
        P(("rows", "pair"), None),
        P(("rows", "pair")),
        P("rows", None),
    )
    out_specs = P("rows", None, None, None)
    return jax.shard_map(
        functools.partial(shards, DIMS),
        mesh=mesh,
        in_specs=in_specs,
        out_specs=out_specs,
        check_vma=False,
    )
```

```python
import functools

import jax
import jax.numpy as jnp
from jax import lax
from jax.experimental import pallas as pl
from jax.experimental.pallas import tpu as pltpu
from jax.sharding import PartitionSpec as P

BS = 64
KA = 27
KC = 8
FB = 24
CB = 4
MOST = 4
ROWS = CB * BS
COLS = KC * BS
HALF = COLS // 2
KT = 7
SKEW = 25
PIECES = 1
SENDS = 32
TOGETHER = 12
DIMS = (8, 4, 4)
MESH = pl.DeviceIdType.MESH
BF16 = jnp.bfloat16
F32 = jnp.float32


def fold_blocks(one, two, low):
    top = jnp.where(low, one, pltpu.roll(two, BS, 1))
    bottom = jnp.where(low, pltpu.roll(one, BS, 1), two)
    return top, bottom


def low_lanes():
    return lax.broadcasted_iota(jnp.int32, (32, 128), 1) < BS


def relay_a(g, a_ref, stage, left):
    low = low_lanes()
    for half in range(2):
        for t in range(32):
            stage[half, pl.ds(t * SKEW, FB), :] = a_ref[
                jnp.minimum(2 * g + half, KA - 1), :, pl.ds(t * 128, 128)
            ].astype(F32)
    column = pl.ds(pl.multiple_of(g * 128, 128), 128)
    for f in range(FB):
        one = stage[0, pl.ds(f, 32, stride=SKEW), :]
        two = stage[1, pl.ds(f, 32, stride=SKEW), :]
        top, bottom = fold_blocks(one, two, low)
        left[f, pl.ds(0, 32), column] = top.astype(BF16)
        left[f, pl.ds(32, 32), column] = bottom.astype(BF16)


def relay_p(w, keep, praw, stage, nat, window, qperm):
    low = low_lanes()
    for t in range(32):
        stage[0, pl.ds(t * SKEW, FB), :] = praw[w, :, pl.ds(t * 128, 128)].astype(F32)
    for b in range(FB):
        one = stage[0, pl.ds(b, 32, stride=SKEW), :]
        top, bottom = fold_blocks(one, one, low)
        if keep:
            qperm[pl.ds(b * BS, 32), :] = top
            qperm[pl.ds(b * BS + 32, 32), :] = bottom
        nat[b % 4, pl.ds(0, 32, stride=2), :] = top
        nat[b % 4, pl.ds(1, 32, stride=2), :] = bottom
        window[w * FB + b] = nat[b % 4].astype(BF16)


def fill_masks(slot_mask, side_mask):
    column_slot = lax.broadcasted_iota(jnp.int32, (16, HALF), 1) // BS
    first = lax.broadcasted_iota(jnp.int32, (16, 128), 1) < BS
    for s in range(KC):
        slot_mask[s] = jnp.where(column_slot == s % 4, 1.0, 0.0).astype(BF16)
        for t in range(KC):
            below = jnp.where(first, 1.0 - s // 4, 1.0 - t // 4)
            side_mask[KC * s + t, :, 0:128] = below.astype(BF16)
            side_mask[KC * s + t, :, 128:256] = (1.0 - below).astype(BF16)


def spread(i, n):
    return n // 2 + (i + 1) // 2 * (1 - 2 * (i % 2))


def plane_order(dims, z, own):
    nz, nx, ny = dims
    half = nz // 2
    side = (z // half + 1 - own) % 2
    return [(side * half + (z + own + i) % half) * (nx * ny) for i in range(half)]


def column_order(i, dims, x, y):
    nz, nx, ny = dims
    return (x + spread(i // ny, nx)) % nx * ny + (y + spread(i % ny, ny)) % ny


def fill_onehot(dims, place_of, owner_ref, onehot):
    nz, nx, ny = dims
    z, x, y = place_of
    owner_row = jnp.broadcast_to(owner_ref[...].astype(F32), (128, ROWS))
    owners = jnp.transpose(owner_row)
    target = jnp.where(
        owners == lax.broadcasted_iota(jnp.int32, (ROWS, 128), 1).astype(F32), 1.0, 0.0
    )
    earlier = jnp.where(
        lax.broadcasted_iota(jnp.int32, (ROWS, ROWS), 0)
        > lax.broadcasted_iota(jnp.int32, (ROWS, ROWS), 1),
        1.0,
        0.0,
    ).astype(BF16)
    before = jnp.dot(earlier, target.astype(BF16), preferred_element_type=F32)
    rank = jnp.sum(before * target, axis=1, keepdims=True)
    key_row = jnp.transpose(owners * MOST + rank)[0:1, :]
    slot = lax.broadcasted_iota(jnp.int32, (16, ROWS), 0) % MOST
    upper = lax.broadcasted_iota(jnp.int32, (16, ROWS), 0) // 8
    half = nz // 2

    def column(own, planes, i, carry):
        there = column_order(i, dims, x, y)
        for u in range(0, half, 2):
            code = slot + (planes[u] + there) * MOST + upper * ((planes[u + 1] - planes[u]) * MOST)
            rows = pl.ds(pl.multiple_of(((own * nx * ny + i) * half + u) * 8, 16), 16)
            onehot[rows, :] = jnp.where(code.astype(F32) == key_row, 1.0, 0.0).astype(BF16)
        return carry

    for own in range(2):
        planes = plane_order(dims, z, own)
        lax.fori_loop(0, nx * ny, functools.partial(column, own, planes), 0)


def fill_turned(chip, agg_ref, qperm, turned):
    wide = lax.broadcasted_iota(jnp.int32, (128, 128), 1) < BS
    tall = lax.broadcasted_iota(jnp.int32, (128, 128), 0) // BS
    for g in range(FB // 2):
        block = jnp.transpose(qperm[pl.ds(g * 128, 128), :])
        member = jnp.where(wide, agg_ref[2 * g], agg_ref[2 * g + 1]) - chip * CB
        for u in range(CB // 2):
            turned[pl.ds(u * 128, 128), pl.ds(g * 128, 128)] = jnp.where(
                member == tall + 2 * u, block, 0.0
            ).astype(BF16)


def tall(mask):
    return jnp.concatenate([mask] * (BS // 16), axis=0)


def positions(f, kk, base, cols_ref, slots_ref, left, window, slot_mask, side_mask):
    blocks, low, high = [], [], []
    for k in (4 * kk, 4 * kk + 2):
        slots = [slots_ref[f, min(k + i, KA - 1)] for i in range(2)]
        for i in range(2):
            if k + i < KA:
                block = window[jnp.clip(cols_ref[f, k + i] - base, 0, 3 * FB - 1)]
                keep = tall(slot_mask[slots[i]])
                blocks.append(jnp.concatenate([block, block], axis=1) * keep)
            else:
                blocks.append(jnp.zeros((BS, HALF), BF16))
        pair = left[f, :, pl.ds(k * BS, 128)]
        keep = side_mask[slots[0] * KC + slots[1]]
        low.append(pair * tall(keep[:, 0:128]))
        high.append(pair * tall(keep[:, 128:256]))
    rows = [jnp.concatenate(low, axis=1), jnp.concatenate(high, axis=1)]
    return jnp.dot(
        jnp.concatenate(rows, axis=0),
        jnp.concatenate(blocks, axis=0),
        preferred_element_type=F32,
    )


def fine_rows(g, base, cols_ref, slots_ref, left, window, slot_mask, side_mask, summed):
    total = [None] * TOGETHER
    for kk in range(KT):
        for i in range(TOGETHER):
            f = g * TOGETHER + i
            term = positions(
                f, kk, base, cols_ref, slots_ref, left, window, slot_mask, side_mask
            )
            total[i] = term if kk == 0 else total[i] + term
    for i in range(TOGETHER):
        rows = pl.ds(pl.multiple_of((g * TOGETHER + i) * BS, BS), BS)
        summed[rows, 0:HALF] = total[i][0:BS].astype(BF16)
        summed[rows, HALF:COLS] = total[i][BS:].astype(BF16)


def place(i, n, whole, onehot, outbox):
    first = (lax.broadcasted_iota(jnp.int32, (8 * n, 128), 0) // MOST) % 2 == 0
    placed = jnp.dot(onehot[pl.ds(i * 8 * n, 8 * n), :], whole, preferred_element_type=F32)
    value = jnp.where(first, placed[:, 0:128], placed[:, 128:256])
    for j in range(n):
        outbox[i * n + j] = value[j * 8 : (j + 1) * 8].astype(BF16)


def kernel(
    dims,
    a_hbm,
    cols_hbm,
    slots_hbm,
    prolong_hbm,
    agg_hbm,
    owner_hbm,
    out_ref,
    cols_ref,
    slots_ref,
    agg_ref,
    owner_ref,
    a_ref,
    praw,
    stage,
    nat,
    left,
    window,
    slot_mask,
    side_mask,
    qperm,
    turned,
    summed,
    onehot,
    part,
    theirs,
    outbox,
    a_sem,
    p_sem,
    small_sem,
    near_send,
    near_recv,
    pair_send,
    pair_recv,
    out_send,
    out_recv,
    fwd_send,
    fwd_recv,
    ring_sem,
):
    nz, nx, ny = dims
    chips = nz * nx * ny
    plane = nx * ny
    chip = lax.axis_index("rows")
    core = lax.axis_index("pair")
    other = 1 - core
    z, x, y = chip // (nx * ny), (chip // ny) % nx, chip % ny
    beyond = chip - 1 + 2 * core
    has_beyond = jnp.logical_and(beyond >= 0, beyond < chips)

    z_ring = [((z + i) % nz * nx + x) * ny + y for i in range(1, nz)]
    x_ring = [(z * nx + (x + i) % nx) * ny + y for i in range(1, nx)]
    y_ring = [(z * nx + x) * ny + (y + i) % ny for i in range(1, ny)]

    def signal_ring(sem, ring):
        for there in ring:
            pl.semaphore_signal(sem, inc=1, device_id=(there, core), device_id_type=MESH)

    barrier = pltpu.get_barrier_semaphore()
    pl.semaphore_signal(barrier, inc=1, device_id=(chip, other), device_id_type=MESH)

    @pl.when(has_beyond)
    def _():
        pl.semaphore_signal(barrier, inc=1, device_id=(beyond, other), device_id_type=MESH)

    signal_ring(barrier, y_ring + x_ring + z_ring)
    fetches = []
    for i in range(KT):
        span = pl.ds(4 * i, min(4, KA - 4 * i))
        fetches.append(pltpu.make_async_copy(a_hbm.at[span], a_ref.at[span], a_sem.at[i]))
    own = pltpu.make_async_copy(prolong_hbm, praw.at[1], p_sem)
    own.start()
    small = [
        pltpu.make_async_copy(src, dst, small_sem.at[i])
        for i, (src, dst) in enumerate(
            [
                (owner_hbm, owner_ref),
                (agg_hbm, agg_ref),
                (cols_hbm, cols_ref),
                (slots_hbm, slots_ref),
            ]
        )
    ]
    for copy in small:
        copy.start()

    fill_masks(slot_mask, side_mask)
    pl.semaphore_wait(
        barrier,
        1 + has_beyond.astype(jnp.int32) + nz + nx + ny - 3,
    )

    own.wait()
    to_partner = pltpu.make_async_remote_copy(
        src_ref=praw.at[1],
        dst_ref=praw.at[2 * core],
        send_sem=near_send.at[0],
        recv_sem=near_recv.at[0],
        device_id=(chip, other),
        device_id_type=MESH,
    )
    to_beyond = pltpu.make_async_remote_copy(
        src_ref=praw.at[1],
        dst_ref=praw.at[2 * other],
        send_sem=near_send.at[1],
        recv_sem=near_recv.at[1],
        device_id=(beyond, other),
        device_id_type=MESH,
    )
    pl.when(has_beyond)(to_beyond.start)
    to_partner.start()
    for fetch in fetches:
        fetch.start()
    signal_ring(ring_sem.at[0], y_ring)

    relay_p(1, True, praw, stage, nat, window, qperm)
    small[1].wait()
    fill_turned(chip, agg_ref, qperm, turned)

    for i in range(KT):
        fetches[i].wait()

        def relay(g, carry):
            relay_a(g, a_ref, stage, left)
            return carry

        lax.fori_loop(2 * i, 2 * i + 2, relay, 0)
        if i == 4:
            to_partner.wait_recv()
            relay_p(2 * other, False, praw, stage, nat, window, qperm)

    pl.semaphore_wait(ring_sem.at[0], ny - 1)
    signal_ring(ring_sem.at[1], x_ring)
    pl.when(has_beyond)(to_beyond.wait_recv)
    relay_p(2 * core, False, praw, stage, nat, window, qperm)

    small[2].wait()
    small[3].wait()
    base = (chip * 2 + core - 1) * FB

    def rows_step(g, carry):
        fine_rows(g, base, cols_ref, slots_ref, left, window, slot_mask, side_mask, summed)
        return carry

    lax.fori_loop(0, FB // TOGETHER, rows_step, 0)
    exchanges = []
    for i, h in enumerate((other, core)):
        for j in range(PIECES):
            rows = pl.ds(j * (ROWS // PIECES), ROWS // PIECES)
            part[i, rows, :] = jnp.dot(
                turned[rows, :],
                summed[:, pl.ds(pl.multiple_of(h * HALF, HALF), HALF)],
                preferred_element_type=F32,
            )
            if i == 0:
                exchange = pltpu.make_async_remote_copy(
                    src_ref=part.at[0, rows],
                    dst_ref=theirs.at[rows],
                    send_sem=pair_send.at[j],
                    recv_sem=pair_recv.at[j],
                    device_id=(chip, other),
                    device_id_type=MESH,
                )
                exchange.start()
                exchanges.append(exchange)

    span = nz // 2

    def column(own, planes, i, carry):
        there = column_order(i, dims, x, y)
        for u in range(span):

            def send(u=u):
                pltpu.make_async_remote_copy(
                    src_ref=outbox.at[(own * plane + i) * span + u],
                    dst_ref=out_ref.at[chip, core],
                    send_sem=out_send,
                    recv_sem=out_recv.at[z],
                    device_id=(planes[u] + there, core),
                    device_id_type=MESH,
                ).start()

            if own == 0 or u < span - 1:
                send()
            else:
                pl.when(i < plane - 1)(send)
        return carry

    small[0].wait()
    fill_onehot(dims, (z, x, y), owner_ref, onehot)
    pl.semaphore_wait(ring_sem.at[1], nx - 1)
    for exchange in exchanges:
        exchange.wait_recv()
    whole = (part[1] + theirs[...]).astype(BF16)
    n = min(SENDS, chips)
    for i in range(chips // n):
        place(i, n, whole, onehot, outbox)
        own, first = divmod(i * n // span, plane)
        step = functools.partial(column, own, plane_order(dims, z, own))
        lax.fori_loop(first, first + n // span, step, 0)
    last = chips - 1
    pltpu.make_async_copy(outbox.at[last], out_ref.at[chip, core], out_recv.at[z]).start()

    forwards = []
    for i in range(nz):
        there = (z + i) % nz
        arrived = out_ref.at[pl.ds(there * plane, plane), core]
        pltpu.make_async_copy(arrived, arrived, out_recv.at[there]).wait()
        forward = pltpu.make_async_remote_copy(
            src_ref=arrived,
            dst_ref=arrived,
            send_sem=fwd_send.at[there],
            recv_sem=fwd_recv.at[there],
            device_id=(chip, other),
            device_id_type=MESH,
        )
        forward.start()
        forwards.append(forward)
    sent = outbox.at[pl.ds(0, chips - 1)]
    pltpu.make_async_copy(sent, sent, out_send).wait()
    to_partner.wait_send()
    pl.when(has_beyond)(to_beyond.wait_send)
    for exchange in exchanges:
        exchange.wait_send()
    for i in range(nz):
        forwards[i].wait_send()
        theirs_there = out_ref.at[pl.ds((z + i) % nz * plane, plane), other]
        pltpu.make_async_copy(theirs_there, theirs_there, fwd_recv.at[(z + i) % nz]).wait()


def shards(dims, a_blocks, a_cols, slots, prolong, aggregate, owner):
    chips = dims[0] * dims[1] * dims[2]
    hbm = pl.BlockSpec(memory_space=pltpu.HBM)
    vmem = pl.BlockSpec(memory_space=pltpu.VMEM)
    dma = pltpu.SemaphoreType.DMA
    arrived = pl.pallas_call(
        functools.partial(kernel, dims),
        out_shape=jax.ShapeDtypeStruct((chips, 2, 8, 128), BF16),
        in_specs=[hbm] * 6,
        out_specs=vmem,
        scratch_shapes=[
            pltpu.SMEM((FB, KA), jnp.int32),
            pltpu.SMEM((FB, KA), jnp.int32),
            pltpu.SMEM((FB,), jnp.int32),
            pltpu.VMEM((1, ROWS), jnp.int32),
            pltpu.VMEM((KA, FB, BS * BS), BF16),
            pltpu.VMEM((3, FB, BS * BS), BF16),
            pltpu.VMEM((2, 32 * 32, 128), F32),
            pltpu.VMEM((4, BS, 128), F32),
            pltpu.VMEM((FB, BS, KT * 256), BF16),
            pltpu.VMEM((3 * FB, BS, 128), BF16),
            pltpu.VMEM((KC, 16, HALF), BF16),
            pltpu.VMEM((KC * KC, 16, HALF), BF16),
            pltpu.VMEM((FB * BS, 128), F32),
            pltpu.VMEM((ROWS, FB * BS), BF16),
            pltpu.VMEM((FB * BS, COLS), BF16),
            pltpu.VMEM((chips * 8, ROWS), BF16),
            pltpu.VMEM((2, ROWS, HALF), F32),
            pltpu.VMEM((ROWS, HALF), F32),
            pltpu.VMEM((chips, 8, 128), BF16),
            dma((KT,)),
            dma,
            dma((4,)),
            dma((2,)),
            dma((2,)),
            dma((PIECES,)),
            dma((PIECES,)),
            dma,
            dma((dims[0],)),
            dma((dims[0],)),
            dma((dims[0],)),
            pltpu.SemaphoreType.REGULAR((2,)),
        ],
        compiler_params=pltpu.CompilerParams(
            collective_id=0, has_side_effects=True, vmem_limit_bytes=48 * 1024 * 1024
        ),
    )(
        *[
            pltpu.with_memory_space_constraint(x, pltpu.HBM)
            for x in (
                jnp.transpose(a_blocks, (1, 0, 2)),
                a_cols,
                slots,
                prolong,
                aggregate,
                owner.reshape(1, ROWS),
            )
        ]
    )
    rows = arrived.reshape(chips, 4, MOST, 128).astype(F32)
    return jnp.transpose(rows, (0, 2, 1, 3)).reshape(1, chips, MOST, COLS)


def solution(mesh):
    in_specs = (
        P(("rows", "pair"), None, None),
        P(("rows", "pair"), None),
        P(("rows", "pair"), None),
        P(("rows", "pair"), None),
        P(("rows", "pair")),
        P("rows", None),
    )
    out_specs = P("rows", None, None, None)
    return jax.shard_map(
        functools.partial(shards, DIMS),
        mesh=mesh,
        in_specs=in_specs,
        out_specs=out_specs,
        check_vma=False,
    )
```
